128 devices in a mesh: rep: 8 (over y, core), neg: 16 (over x, z).
Axes of the slice: x: 4, y: 4, z: 4, core: 2. Of those that a mesh axis runs over, the one named last changes fastest.
Arguments:
- feature_table: bfloat16 [131072, 1024], P(('rep', 'neg')), may hold values from -6 to 6
- cur_rows: bfloat16 [98304, 1024], P(('rep', 'neg')), may hold values from -6 to 6
- next_owner: int32 [98304, 1], P(('rep', 'neg')), may hold values from 0 to 127; in each aligned block of 768 rows (0 to 767, 768 to 1535, ...) at most 12 rows name the same one
- next_local: int32 [98304], P(('rep', 'neg')), may hold values from 0 to 1023
- slot_counts: int32 [6144, 16], P(('rep', 'neg')), may hold values from 0 to 63, as said below
- hop_counts: int32 [512, 12], P(('rep', 'neg')), may hold values from 0 to 63, as said below
- positive_ids: int32 [512], P(('rep', 'neg')), may hold values from 0 to 1023
- neighbor_weight: bfloat16 [1024, 2048], replicated, may hold values from -0.1875 to 0.1875
- combine_weight: bfloat16 [3072, 2048], replicated, may hold values from -0.109375 to 0.109375
- candidates: bfloat16 [8192, 2048], P(('rep', 'neg')), may hold values from -0.296875 to 0.296875
Outputs:
- next_rows: bfloat16 [98304, 1024], P(('rep', 'neg'))
- query_loss: float32 [512], P(('rep', 'neg'))
- cand_grad: float32 [8192, 2048], P(('rep', 'neg'))
- neighbor_grad: float32 [1024, 2048], P(('rep', 'neg'))
The draws below stay inside these ranges and needn't reach their ends.
Inputs may be any that keep to these rules, and one draw needn't show every extreme that they name: `next_owner`: among the 768 rows of one device no owner is named more than 12 times. `slot_counts`: 0 marks a padded slot; slot 0, the node itself, is at least 1. `hop_counts`: 0 marks a padded slot; the first is at least 1.
All inputs are finite; a program needn't handle non-finite values.
Results may differ from the reference program's by a relative error of at most 0.011.
The reference program's roundings to bfloat16 on the way (of `pooled_low`, `embedding`, `score_grad`, `mixed_in_grad` and `projected_grad`) count: a program that leaves them out, or rounds other values in their place, can miss the bound.
Values may be sent and summed in bfloat16 or wider, within the bound.
A program may use at most 128 MiB of HBM per device.

```python
import math
import jax
import jax.numpy as jnp
import numpy as np
from jax import lax

F = 1024
H = 2048
B = 4
K1 = 12
SLOTS = 16
TABLE_DEV = 1024
CAND_DEV = 64
HOP1 = 48
REQ = 768
CAP = 12
CANDS = 1024
QUERIES = 512
ALL_HOP1 = 6144
N_REP = 8
N_NEG = 16
DEVICES = 128


def visit_counts(key, row_count, column_count):
    first_key, pad_key, value_key = jax.random.split(key, 3)
    first = jax.random.randint(first_key, (row_count, 1), 1, 64)
    padded = jax.random.randint(pad_key, (row_count, column_count - 1), 0, 4) == 0
    values = jax.random.randint(value_key, (row_count, column_count - 1), 1, 64)
    others = jnp.where(padded, 0, values)
    return jnp.concatenate([first, others], axis=1).astype(jnp.int32)


def target_rows(jitter, offset_key, strength):
    offset = jax.random.normal(offset_key, (jitter.shape[0], 1, jitter.shape[2]), jnp.float32)
    result_rows = (jitter + strength * offset) / math.sqrt(1.0 + strength * strength)
    result_rows = jnp.clip(result_rows, -6.0, 6.0)
    return result_rows.reshape(jitter.shape[0] * jitter.shape[1], jitter.shape[2]).astype(jnp.bfloat16)


def draw_cur_rows(key, part):
    key = jax.random.fold_in(key, 37)
    jitter_key, offset_key = jax.random.split(key)
    group_size = K1 * SLOTS
    jitter = jax.random.normal(jitter_key, (QUERIES, group_size, F), jnp.float32)
    return target_rows(jitter, offset_key, 2.0)


def draw_slot_counts(key, part):
    key = jax.random.fold_in(key, 11)
    return visit_counts(key, ALL_HOP1, SLOTS)


def draw_hop_counts(key, part):
    key = jax.random.fold_in(key, 23)
    return visit_counts(key, QUERIES, K1)


def place_ends(drawn, own_key, least, largest):
    spot = [jax.random.randint(jax.random.fold_in(own_key, axis), (), 0, length) for axis, length in enumerate(drawn.shape)]
    main_axis = drawn.shape.index(max(drawn.shape))
    next_to = spot[:main_axis] + [(spot[main_axis] + 1) % drawn.shape[main_axis]] + spot[main_axis + 1:]
    return drawn.at[tuple(spot)].set(least).at[tuple(next_to)].set(largest)


def block_scale(key, dims, shards, smallest, largest):
    level, own = 1.0, jax.random.fold_in(key, 6)
    for dim, shards_of in shards:
        heights = jnp.exp(jax.random.uniform(jax.random.fold_in(own, dim), (shards_of,), jnp.float32, smallest / len(shards), largest / len(shards)))
        level = level * jnp.repeat(heights, dims[dim] // shards_of).reshape([-1 if axis == dim else 1 for axis in range(len(dims))])
    return level


def shared_out(key, own, number, rows, amount, top, most, skew):
    sequence = jax.random.permutation(key, amount)
    heavy_load, common = portions_of(amount, rows * top, most, skew, True), portions_of(amount, rows * top, most, skew, False)
    places = jnp.arange(amount)

    def named(tallies, rotation):
        used = int((tallies > 0).sum())
        fixed = max(1, used // 4)
        moved = fixed + (places - fixed + rotation * (used - fixed)) % max(1, amount - fixed)
        return jnp.zeros((amount,), jnp.int32).at[sequence[jnp.where(places < fixed, places, moved)]].set(jnp.asarray(tallies, jnp.int32))

    tallies = jnp.where(number % 4 == 0, named(heavy_load, number // 4), named(common, number - number // 4 - 1))
    mixed = jax.random.permutation(jax.random.fold_in(own, 3), amount)
    donor, receiver = mixed[0:amount // 2 * 2:2], mixed[1:amount // 2 * 2:2]
    margin = jnp.minimum(tallies[donor] - 1, most - tallies[receiver]) // 2
    margin = jnp.where((donor == sequence[0]) | (receiver == sequence[0]) | (tallies[receiver] == 0), 0, jnp.maximum(margin, 0))
    moved = jax.random.randint(jax.random.fold_in(own, 4), (amount // 2,), 0, 1 << 20) % (margin + 1)
    tallies = tallies.at[donor].add(-moved).at[receiver].add(moved)
    members = jnp.searchsorted(jnp.cumsum(tallies), jnp.arange(rows * top), side="right").astype(jnp.int32)
    grid = members.reshape(top, rows).T
    grid = grid[jax.random.permutation(jax.random.fold_in(own, 1), rows)]
    rotation = jax.random.randint(jax.random.fold_in(own, 2), (rows, 1), 0, top)
    return jnp.take_along_axis(grid, (jnp.arange(top)[None, :] + rotation) % top, axis=1)


def portions_of(amount, total, most, lean, full):
    weights = [(1 << 20) // math.isqrt(standing ** lean) + 1 for standing in range(1, amount + 1)]
    largest = most if full else min(most, max(-(-total // amount), total * weights[0] // sum(weights)))
    least = 1 if total - largest >= amount - 1 else 0
    counts, spare = [largest] + [least] * (amount - 1), total - largest - least * (amount - 1)
    while spare > 0:
        free = [i for i in range(1, amount) if counts[i] < largest] or [i for i in range(1, amount) if counts[i] < most]
        mass, left = sum([weights[i] for i in free]), spare
        for i in free:
            more = min(most - counts[i], max(1, left * weights[i] // mass), spare)
            counts[i] = counts[i] + more
            spare = spare - more
    return np.array(counts)


def normal_values(own_key, shape, spread, limit, cuts=(), kind=jnp.bfloat16):
    gain = block_scale(own_key, shape, cuts, -0.22, 0.18) if cuts else 1.0
    drawn = jax.random.normal(own_key, shape, jnp.float32) * spread * gain
    return jnp.minimum(jnp.maximum(drawn, -limit), limit).astype(kind)


def setup_inputs(seed: int = 0) -> dict:
    splits = jax.random.split(jax.random.key(seed), 11)
    feature_table = normal_values(splits[0], (TABLE_DEV * DEVICES, F), 1.0, 6.0, ((0, 128),))
    cur_rows = draw_cur_rows(jax.random.fold_in(splits[10], 71), 0)
    next_owner_keys = jax.random.split(jax.random.fold_in(splits[2], 1), (DEVICES * REQ) // REQ)
    next_owner_turns = jax.random.permutation(jax.random.fold_in(splits[2], 3), (DEVICES * REQ) // REQ)
    next_owner = jax.vmap(lambda own, number: shared_out(jax.random.fold_in(splits[2], 2), own, number, REQ, DEVICES, 1, CAP, 1))(next_owner_keys, next_owner_turns).reshape((DEVICES * REQ, 1))
    next_local = place_ends(jax.random.randint(splits[3], (DEVICES * REQ,), 0, TABLE_DEV), jax.random.fold_in(splits[3], 1), 0, TABLE_DEV - 1).astype(jnp.int32)
    slot_counts = draw_slot_counts(jax.random.fold_in(splits[10], 71), 0)
    hop_counts = draw_hop_counts(jax.random.fold_in(splits[10], 71), 0)
    positive_ids = place_ends(jax.random.randint(splits[6], (QUERIES,), 0, CANDS), jax.random.fold_in(splits[6], 1), 0, CANDS - 1).astype(jnp.int32)
    neighbor_weight = normal_values(splits[7], (F, H), F ** -0.5, 0.1875)
    combine_weight = normal_values(splits[8], (F + H, H), (F + H) ** -0.5, 0.109375)
    candidates = jnp.clip(jax.random.uniform(splits[9], (CAND_DEV * DEVICES, H), jnp.float32, -0.296875, 0.296875) * block_scale(splits[9], (CAND_DEV * DEVICES, H), ((0, 128),), -0.4, 0.0), -0.296875, 0.296875).astype(jnp.bfloat16)
    return dict(feature_table=feature_table, cur_rows=cur_rows, next_owner=next_owner, next_local=next_local, slot_counts=slot_counts, hop_counts=hop_counts, positive_ids=positive_ids, neighbor_weight=neighbor_weight, combine_weight=combine_weight, candidates=candidates)


EPSILON = 1e-06
MARGIN = 0.5

def rms_scale(values):
    return values * lax.rsqrt(lax.optimization_barrier(jnp.mean(values * values, axis=-1, keepdims=True)) + EPSILON)

def forward_device(row_block, slot_block, hop_block, neighbor_weight, combine_weight):
    projected = jnp.dot(row_block, neighbor_weight, preferred_element_type=jnp.float32)
    activated = jnp.maximum(projected, 0.0)
    slot_weight = slot_block.astype(jnp.float32) / lax.optimization_barrier(jnp.sum(slot_block, axis=1, keepdims=True)).astype(jnp.float32)
    pooled = lax.optimization_barrier(jnp.sum(slot_weight[:, :, None] * activated.reshape(HOP1, SLOTS, H), axis=1))
    pooled_low = pooled.astype(jnp.bfloat16)
    self_rows = row_block.reshape(HOP1, SLOTS, F)[:, 0, :]
    mixed_in = jnp.dot(self_rows, combine_weight[:F], preferred_element_type=jnp.float32)
    mixed_in = mixed_in + jnp.dot(pooled_low, combine_weight[F:], preferred_element_type=jnp.float32)
    mixed = jnp.maximum(mixed_in, 0.0)
    normed = rms_scale(mixed)
    hop_weight = hop_block.astype(jnp.float32) / lax.optimization_barrier(jnp.sum(hop_block, axis=1, keepdims=True)).astype(jnp.float32)
    top_in = lax.optimization_barrier(jnp.sum(hop_weight[:, :, None] * normed.reshape(B, K1, H), axis=1))
    embedding = rms_scale(top_in).astype(jnp.bfloat16)
    return (embedding, (projected, slot_weight, mixed_in, mixed, hop_weight, top_in))

def backward_device(row_block, slot_block, hop_block, neighbor_weight, combine_weight, embed_grad):
    unused, saved = forward_device(row_block, slot_block, hop_block, neighbor_weight, combine_weight)
    projected, slot_weight, mixed_in, mixed, hop_weight, top_in = saved
    unused_top, top_back = jax.vjp(rms_scale, top_in)
    top_grad = top_back(embed_grad)[0]
    normed_grad = (hop_weight[:, :, None] * top_grad[:, None, :]).reshape(HOP1, H)
    unused_mid, mid_back = jax.vjp(rms_scale, mixed)
    mixed_grad = mid_back(normed_grad)[0]
    mixed_in_grad = jnp.where(mixed_in > 0.0, mixed_grad, 0.0).astype(jnp.bfloat16)
    pooled_grad = lax.dot_general(mixed_in_grad, combine_weight[F:], (((1,), (1,)), ((), ())), preferred_element_type=jnp.float32)
    activated_grad = (slot_weight[:, :, None] * pooled_grad[:, None, :]).reshape(REQ, H)
    projected_grad = jnp.where(projected > 0.0, activated_grad, 0.0).astype(jnp.bfloat16)
    return lax.dot_general(row_block, projected_grad, (((0,), (0,)), ((), ())), preferred_element_type=jnp.float32)

def score_group(embeds, group_cands, positives):
    scores = lax.dot_general(embeds, group_cands, (((1,), (1,)), ((), ())), preferred_element_type=jnp.float32)
    positive_score = jnp.take_along_axis(scores, positives[:, None], axis=1)
    gaps = scores - positive_score + MARGIN
    query_loss = lax.optimization_barrier(jnp.mean(jax.nn.softplus(gaps), axis=1))
    sigmoid_gaps = jax.nn.sigmoid(gaps)
    totals = lax.optimization_barrier(jnp.sum(sigmoid_gaps, axis=1, keepdims=True))
    chosen = jnp.arange(CANDS, dtype=jnp.int32)[None, :] == positives[:, None]
    score_grad = ((sigmoid_gaps - jnp.where(chosen, totals, 0.0)) / CANDS).astype(jnp.bfloat16)
    cand_grad = lax.dot_general(score_grad, embeds, (((0,), (0,)), ((), ())), preferred_element_type=jnp.float32)
    embed_grad = jnp.dot(score_grad, group_cands, preferred_element_type=jnp.float32)
    return (query_loss, cand_grad, embed_grad)

def reference(feature_table, cur_rows, next_owner, next_local, slot_counts, hop_counts, positive_ids, neighbor_weight, combine_weight, candidates):
    devices = N_REP * N_NEG
    next_rows = feature_table[next_owner[:, 0] * TABLE_DEV + next_local]
    row_blocks = cur_rows.reshape(devices, REQ, F)
    slot_blocks = slot_counts.reshape(devices, HOP1, SLOTS)
    hop_blocks = hop_counts.reshape(devices, B, K1)

    def embed_one(inputs):
        return forward_device(inputs[0], inputs[1], inputs[2], neighbor_weight, combine_weight)[0]
    embeds = lax.map(embed_one, (row_blocks, slot_blocks, hop_blocks))
    group_embeds = embeds.reshape(N_REP, N_NEG * B, H)
    group_cands = candidates.reshape(N_REP, CANDS, H)
    group_pos = positive_ids.reshape(N_REP, N_NEG * B)

    def score_one(inputs):
        return score_group(inputs[0], inputs[1], inputs[2])
    query_loss, cand_grad, embed_grad = lax.map(score_one, (group_embeds, group_cands, group_pos))
    embed_grad = embed_grad.reshape(devices, B, H)

    def accumulate(total, inputs):
        term = backward_device(inputs[0], inputs[1], inputs[2], neighbor_weight, combine_weight, inputs[3])
        return (total + term, None)
    neighbor_grad, unused = lax.scan(accumulate, jnp.zeros((F, H), jnp.float32), (row_blocks, slot_blocks, hop_blocks, embed_grad))
    return (next_rows, query_loss.reshape(QUERIES), cand_grad.reshape(N_REP * CANDS, H), neighbor_grad)
```

```python
import jax
import jax.numpy as jnp
from jax import lax
from jax.sharding import PartitionSpec as P

EPSILON = 1e-06
MARGIN = 0.5


def rms_scale(values):
    return values * lax.rsqrt(jnp.mean(values * values, axis=-1, keepdims=True) + EPSILON)


def local(
    feature_table,
    cur_rows,
    next_owner,
    next_local,
    slot_counts,
    hop_counts,
    positive_ids,
    neighbor_weight,
    combine_weight,
    candidates,
):
    devices = lax.axis_size(("rep", "neg"))
    request_count = cur_rows.shape[0]
    feature = cur_rows.shape[1]
    width = neighbor_weight.shape[1]
    hop_rows = slot_counts.shape[0]
    slot_count = slot_counts.shape[1]
    batch = hop_counts.shape[0]
    fanout = hop_counts.shape[1]
    capacity = 2 * request_count // devices
    owner_ids = next_owner[:, 0]
    owner_hits = (owner_ids[:, None] == jnp.arange(devices, dtype=jnp.int32)[None, :]).astype(
        jnp.int32
    )
    slot_rank = jnp.sum((jnp.cumsum(owner_hits, axis=0) - 1) * owner_hits, axis=1)
    requests = jnp.full((devices, capacity), -1, jnp.int32).at[owner_ids, slot_rank].set(next_local)
    asked = lax.all_to_all(requests, ("rep", "neg"), split_axis=0, concat_axis=0, tiled=True)
    present = asked >= 0
    fetched = feature_table.reshape(-1, 8, feature // 8)[jnp.maximum(asked, 0)]
    returned = lax.all_to_all(
        jnp.where(present[..., None, None], fetched, jnp.zeros_like(fetched)),
        ("rep", "neg"),
        split_axis=0,
        concat_axis=0,
        tiled=True,
    )
    next_rows = returned[owner_ids, slot_rank].reshape(request_count, feature)
    cand_all = lax.all_gather(candidates, "neg", axis=0, tiled=True)
    cand_total = cand_all.shape[0]
    projected = jnp.dot(cur_rows, neighbor_weight, preferred_element_type=jnp.float32)
    activated = jnp.maximum(projected, 0.0)
    slot_weight = slot_counts.astype(jnp.float32) / jnp.sum(
        slot_counts, axis=1, keepdims=True
    ).astype(jnp.float32)
    pooled = jnp.sum(
        slot_weight[:, :, None] * activated.reshape(hop_rows, slot_count, width), axis=1
    )
    pooled_low = pooled.astype(jnp.bfloat16)
    self_rows = cur_rows.reshape(hop_rows, slot_count, feature)[:, 0, :]
    mixed_in = jnp.dot(self_rows, combine_weight[:feature], preferred_element_type=jnp.float32)
    mixed_in = mixed_in + jnp.dot(
        pooled_low, combine_weight[feature:], preferred_element_type=jnp.float32
    )
    mixed = jnp.maximum(mixed_in, 0.0)
    normed = rms_scale(mixed)
    hop_weight = hop_counts.astype(jnp.float32) / jnp.sum(hop_counts, axis=1, keepdims=True).astype(
        jnp.float32
    )
    top_in = jnp.sum(hop_weight[:, :, None] * normed.reshape(batch, fanout, width), axis=1)
    embedding = rms_scale(top_in).astype(jnp.bfloat16)
    scores = lax.dot_general(
        embedding, cand_all, (((1,), (1,)), ((), ())), preferred_element_type=jnp.float32
    )
    positive_score = jnp.take_along_axis(scores, positive_ids[:, None], axis=1)
    gaps = scores - positive_score + MARGIN
    query_loss = jnp.mean(jax.nn.softplus(gaps), axis=1)
    sigmoid_gaps = jax.nn.sigmoid(gaps)
    totals = jnp.sum(sigmoid_gaps, axis=1, keepdims=True)
    chosen = jnp.arange(cand_total, dtype=jnp.int32)[None, :] == positive_ids[:, None]
    score_grad = ((sigmoid_gaps - jnp.where(chosen, totals, 0.0)) / cand_total).astype(jnp.bfloat16)
    own = candidates.shape[0]
    grad_split = score_grad.reshape(batch, cand_total // own, own)
    grad_all = lax.all_to_all(grad_split, "neg", split_axis=1, concat_axis=0, tiled=True)
    embed_all = lax.all_gather(embedding, "neg", axis=0, tiled=True)
    cand_grad = lax.dot_general(
        grad_all.reshape(cand_total // own * batch, own),
        embed_all,
        (((0,), (0,)), ((), ())),
        preferred_element_type=jnp.float32,
    )
    embed_grad = jnp.dot(score_grad, cand_all, preferred_element_type=jnp.float32)
    unused_top, top_back = jax.vjp(rms_scale, top_in)
    top_grad = top_back(embed_grad)[0]
    normed_grad = (hop_weight[:, :, None] * top_grad[:, None, :]).reshape(hop_rows, width)
    unused_mid, mid_back = jax.vjp(rms_scale, mixed)
    mixed_grad = mid_back(normed_grad)[0]
    mixed_in_grad = jnp.where(mixed_in > 0.0, mixed_grad, 0.0).astype(jnp.bfloat16)
    pooled_grad = lax.dot_general(
        mixed_in_grad,
        combine_weight[feature:],
        (((1,), (1,)), ((), ())),
        preferred_element_type=jnp.float32,
    )
    activated_grad = (slot_weight[:, :, None] * pooled_grad[:, None, :]).reshape(
        request_count, width
    )
    projected_grad = jnp.where(projected > 0.0, activated_grad, 0.0).astype(jnp.bfloat16)
    partial = lax.dot_general(
        cur_rows, projected_grad, (((0,), (0,)), ((), ())), preferred_element_type=jnp.float32
    )
    reps, negs = lax.axis_size("rep"), lax.axis_size("neg")
    partial = partial.reshape(reps, negs, feature // devices, width).swapaxes(0, 1)
    partial = lax.psum_scatter(
        partial.reshape(feature, width), "neg", scatter_dimension=0, tiled=True
    )
    neighbor_grad = lax.psum_scatter(partial, "rep", scatter_dimension=0, tiled=True)
    return (next_rows, query_loss, cand_grad, neighbor_grad)


def solution(mesh):
    return jax.shard_map(
        local,
        mesh=mesh,
        in_specs=(
            P(("rep", "neg"), None),
            P(("rep", "neg"), None),
            P(("rep", "neg"), None),
            P(("rep", "neg")),
            P(("rep", "neg"), None),
            P(("rep", "neg"), None),
            P(("rep", "neg")),
            P(),
            P(),
            P(("rep", "neg"), None),
        ),
        out_specs=(
            P(("rep", "neg"), None),
            P(("rep", "neg")),
            P(("rep", "neg"), None),
            P(("rep", "neg"), None),
        ),
        check_vma=False,
    )
```

```python
import jax
import jax.numpy as jnp
from jax import lax
from jax.experimental import pallas as pl
from jax.experimental.pallas import tpu as pltpu
from jax.sharding import PartitionSpec as P

EPSILON = 1e-06
MARGIN = 0.5
MESH = pl.DeviceIdType.MESH
F32 = jnp.float32
BF16 = jnp.bfloat16
HIGH = lax.Precision.HIGHEST

REPS, NEGS, DEVS = 8, 16, 128
YS, CORES = 4, 2
F, H = 1024, 2048
TILE = 256
TILES = H // TILE
REQ, HOP1, SLOTS, B, K1 = 768, 48, 16, 4, 12
WIDE = 768
OWN = 64


def iota(shape, dim):
    return lax.broadcasted_iota(jnp.int32, shape, dim)


def nt(a, b, precision=None):
    return lax.dot_general(
        a, b, (((1,), (1,)), ((), ())), preferred_element_type=F32, precision=precision
    )


def tn(a, b, precision=None):
    return lax.dot_general(
        a, b, (((0,), (0,)), ((), ())), preferred_element_type=F32, precision=precision
    )


def nn(a, b, precision=None):
    return jnp.dot(a, b, preferred_element_type=F32, precision=precision)


def bf(mask):
    return mask.astype(F32).astype(BF16)


def kernel(
    owner_ref, local_ref, slot_ref, hop_ref, pos_ref,
    table_hbm, cur_hbm, nw_hbm, cw_hbm, cand_hbm,
    rows_hbm, loss_ref, cand_out, ngrad_ref,
    cur_v, curt_v, table_v, nw_v, cw_v, cand_v, mask_v, pgrad_v, x_v, mixed_v, pooled_g,
    req_send, req_recv, ids_v, row_send, row_recv, rows_acc, cols_v,
    emb_send, emb_all, e_v, sc_send, sc_all, eg_send, eg_recv,
    p_send, p_recv, p_own, a1_send, a1_recv, a2_f, a2_send, a2_recv,
    b1_f, b1_send, b1_recv, b2_f, b2_send, b2_recv,
    in_sem, out_sem, req_ssem, req_rsem, row_ssem, row_rsem,
    emb_ssem, emb_rsem, sc_ssem, sc_rsem, eg_ssem, eg_rsem,
    p_ssem, p_rsem, a1_ssem, a1_rsem, a2_ssem, a2_rsem, b1_ssem, b1_rsem, b2_ssem, b2_rsem,
):
    rep = lax.axis_index("rep")
    neg = lax.axis_index("neg")
    me = rep * NEGS + neg
    y, core = rep // CORES, rep % CORES

    loads = [
        pltpu.make_async_copy(cur_hbm, cur_v, in_sem.at[0]),
        pltpu.make_async_copy(table_hbm, table_v, in_sem.at[1]),
        pltpu.make_async_copy(cand_hbm, cand_v.at[pl.ds(0, OWN)], in_sem.at[2]),
        pltpu.make_async_copy(cand_hbm, cand_v.at[pl.ds(OWN, OWN)], in_sem.at[3]),
    ]
    nw_loads = [
        pltpu.make_async_copy(
            nw_hbm.at[:, pl.ds(j * TILE, TILE)], nw_v.at[j], in_sem.at[4 + j]
        )
        for j in range(TILES)
    ]
    cw_loads = [
        pltpu.make_async_copy(
            cw_hbm.at[:, pl.ds(j * TILE, TILE)], cw_v.at[j], in_sem.at[12 + j]
        )
        for j in range(TILES)
    ]
    loads[0].start()
    for load in nw_loads:
        load.start()
    for load in loads[1:]:
        load.start()
    for load in cw_loads:
        load.start()

    barrier = pltpu.get_barrier_semaphore()

    def greet(i, carry):
        d = lax.rem(me + i, DEVS)
        pl.semaphore_signal(
            barrier, inc=1, device_id=(d // NEGS, d % NEGS), device_id_type=MESH
        )
        return carry

    lax.fori_loop(1, DEVS, greet, 0)

    hit = owner_ref[...] == iota((DEVS, REQ), 0)
    hit_low = bf(hit)
    before = bf(iota((REQ, REQ), 0) < iota((REQ, REQ), 1))
    count = nn(hit_low, before)
    rank = jnp.sum(jnp.where(hit, count, 0.0), axis=0, keepdims=True)
    local = local_ref[...]
    line = iota((DEVS, REQ), 0).astype(F32)
    pay = jnp.where(line == rank, (local >> 5).astype(F32), 0.0) + jnp.where(
        line == rank + 16.0, (local & 31).astype(F32), 0.0
    )
    asks = nt(hit_low, pay.astype(BF16))
    lane1 = iota((1, 128), 1)
    positives = jnp.zeros((1, 128), jnp.int32)
    for t in range(B):
        value = pos_ref[0, t]
        positives = positives + jnp.where(lane1 == 32 + t, value >> 5, 0)
        positives = positives + jnp.where(lane1 == 36 + t, value & 31, 0)
    asks = asks + positives.astype(F32)
    req_send[...] = asks.reshape(DEVS, 1, 128)
    eye = bf(iota((REQ, REQ), 0) == iota((REQ, REQ), 1))
    pair = jnp.where(iota((16, REQ), 0) == 0, owner_ref[...].astype(F32), rank).astype(BF16)
    cols_v[...] = nt(eye, pair)

    pl.semaphore_wait(barrier, DEVS - 1)

    def ask(i, carry):
        d = lax.rem(me + i, DEVS)
        pltpu.make_async_remote_copy(
            src_ref=req_send.at[d],
            dst_ref=req_recv.at[me],
            send_sem=req_ssem.at[d],
            recv_sem=req_rsem.at[me],
            device_id=(d // NEGS, d % NEGS),
            device_id_type=MESH,
        ).start()
        return carry

    lax.fori_loop(1, DEVS, ask, 0)
    req_recv[me] = req_send[me]

    spread = bf(iota((REQ, HOP1), 0) // SLOTS == iota((REQ, HOP1), 1))
    counts = nt(spread, slot_ref[...].astype(F32).astype(BF16))
    at_slot = iota((REQ, SLOTS), 0) % SLOTS == iota((REQ, SLOTS), 1)
    weight = jnp.sum(jnp.where(at_slot, counts, 0.0), axis=1, keepdims=True) / jnp.sum(
        counts, axis=1, keepdims=True
    )

    loads[0].wait()
    for j in range(TILES):
        nw_loads[j].wait()
        projected = nn(cur_v[...], nw_v[j])
        mask_v[j] = bf(projected > 0.0)
        weighted = jnp.maximum(projected, 0.0) * weight
        pooled = jnp.sum(weighted.reshape(HOP1, SLOTS, TILE), axis=1)
        x_v[:, F + j * TILE : F + (j + 1) * TILE] = pooled.astype(BF16)
    first = bf(iota((HOP1, REQ), 0) * SLOTS == iota((HOP1, REQ), 1))
    x_v[:, 0:F] = nn(first, cur_v[...]).astype(BF16)

    def got_ask(i, carry):
        d = lax.rem(me + i, DEVS)
        pltpu.make_async_remote_copy(
            src_ref=req_send.at[d],
            dst_ref=req_recv.at[d],
            send_sem=req_ssem.at[d],
            recv_sem=req_rsem.at[d],
            device_id=(rep, neg),
            device_id_type=MESH,
        ).wait()
        return carry

    lax.fori_loop(1, DEVS, got_ask, 0)
    ids_v[...] = req_recv[...].reshape(DEVS, 128)
    loads[1].wait()

    def serve(step, carry):
        g = lax.rem(rep + step, REPS)
        base = pl.multiple_of(g * NEGS, NEGS)
        asked = ids_v[pl.ds(base, NEGS), :].astype(BF16)

        def chosen(rows, per, slot_of):
            wide = nn(bf(iota((rows, NEGS), 0) // per % NEGS == iota((rows, NEGS), 1)), asked)
            slot = slot_of(iota((rows, 1), 0))
            at = iota((rows, 128), 1)
            ids = jnp.sum(
                jnp.where(at == slot, wide * 32.0, 0.0) + jnp.where(at == slot + 16, wide, 0.0),
                axis=1,
                keepdims=True,
            )
            return bf(ids == iota((rows, F), 1).astype(F32))

        main = nn(chosen(256, 16, lambda r: r % 16), table_v[:, 0:WIDE]).reshape(NEGS, 16, WIDE)
        tail = nn(
            chosen(384, 8, lambda r: jnp.maximum(r % 8 - 4, 0) * 3 + r // 128),
            table_v[:, WIDE:F],
        )
        high = iota((NEGS, 8, TILE), 1) >= 4
        parts = []
        for c in range(3):
            own = main[:, 8:16, c * TILE : (c + 1) * TILE]
            parts.append(
                jnp.where(high, tail[128 * c : 128 * (c + 1)].reshape(NEGS, 8, TILE), own)
            )
        lower = jnp.concatenate(parts, axis=2)
        block = jnp.concatenate([main[:, 0:8, :], lower], axis=1)
        row_send[pl.ds(base, NEGS)] = block.astype(BF16)

        def post(i, carry):
            n = lax.rem(neg + i, NEGS)
            d = g * NEGS + n

            @pl.when(d != me)
            def _():
                pltpu.make_async_remote_copy(
                    src_ref=row_send.at[d],
                    dst_ref=row_recv.at[me],
                    send_sem=row_ssem.at[d],
                    recv_sem=row_rsem.at[me],
                    device_id=(g, n),
                    device_id_type=MESH,
                ).start()

            return carry

        lax.fori_loop(0, NEGS, post, 0)
        return carry

    lax.fori_loop(0, REPS, serve, 0)
    row_recv[me] = row_send[me]

    x = x_v[...]
    for j in range(TILES):
        cw_loads[j].wait()
        mixed_v[:, j * TILE : (j + 1) * TILE] = nn(x, cw_v[j])
    mixed_in = mixed_v[...]
    mixed = jnp.maximum(mixed_in, 0.0)
    inv_mid = lax.rsqrt(jnp.mean(mixed * mixed, axis=1, keepdims=True) + EPSILON)
    normed = mixed * inv_mid
    top_rows = bf(iota((8, B), 0) == iota((8, B), 1))
    hops = nn(top_rows, hop_ref[...].astype(F32).astype(BF16))
    lanes_of = bf(iota((K1, HOP1), 0) == iota((K1, HOP1), 1) % K1)
    own_hop = iota((8, HOP1), 0) == iota((8, HOP1), 1) // K1
    hop_total = jnp.maximum(jnp.sum(hops, axis=1, keepdims=True), 1.0)
    hop_mat = jnp.where(own_hop, nn(hops.astype(BF16), lanes_of), 0.0) / hop_total
    top_in = nn(hop_mat, normed, HIGH)
    inv_top = lax.rsqrt(jnp.mean(top_in * top_in, axis=1, keepdims=True) + EPSILON)
    embedding = (top_in * inv_top).astype(BF16)
    part = H // 4
    packed = jnp.zeros((16, part), F32)
    for c in range(4):
        move = bf(
            (iota((16, 8), 0) == iota((16, 8), 1) + 4 * c) & (iota((16, 8), 1) < B)
        )
        packed = packed + nn(move, embedding[:, c * part : (c + 1) * part])
    emb_send[...] = packed.astype(BF16)

    def peers(body):
        def step(i, carry):
            body(lax.rem(neg + i, NEGS))
            return carry

        lax.fori_loop(1, NEGS, step, 0)

    def copy_to(src, dst, ssem, rsem, where):
        return pltpu.make_async_remote_copy(
            src_ref=src, dst_ref=dst, send_sem=ssem, recv_sem=rsem,
            device_id=where, device_id_type=MESH,
        )

    peers(
        lambda n: copy_to(
            emb_send, emb_all.at[neg], emb_ssem.at[n], emb_rsem.at[neg], (rep, n)
        ).start()
    )
    emb_all[neg] = emb_send[...]
    for b in range(8):
        curt_v[b % 2, 128 * (b // 2) : 128 * (b // 2) + 128, :] = (
            cur_v[:, 128 * b : 128 * b + 128].astype(F32).T.astype(BF16)
        )
    loads[2].wait()
    loads[3].wait()
    peers(
        lambda n: copy_to(
            emb_send, emb_all.at[n], emb_ssem.at[n], emb_rsem.at[n], (rep, neg)
        ).wait()
    )

    gathered = emb_all[...].reshape(256, part)
    row_q, col_q = iota((64, 256), 0), iota((64, 256), 1)
    for c in range(4):
        move = bf(col_q == (row_q // 4) * 16 + 4 * c + row_q % 4)
        e_v[:, c * part : (c + 1) * part] = nn(move, gathered).astype(BF16)
    left = iota((32, 128), 1) < OWN
    scores = jnp.where(left, nt(e_v[0:32, :], cand_v[...]), nt(e_v[32:64, :], cand_v[...]))
    sc_send[...] = scores
    peers(
        lambda n: copy_to(
            sc_send, sc_all.at[neg], sc_ssem.at[n], sc_rsem.at[neg], (rep, n)
        ).start()
    )
    sc_all[neg] = scores
    mates = ids_v[pl.ds(pl.multiple_of(rep * NEGS, NEGS), NEGS), :].astype(BF16)
    halves = []
    for h in range(2):
        pick = bf(iota((32, NEGS), 0) // B + 8 * h == iota((32, NEGS), 1))
        wide = nn(pick, mates)
        at, t = iota((32, 128), 1), iota((32, 128), 0) % B
        halves.append(
            jnp.sum(
                jnp.where(at == 32 + t, wide * 32.0, 0.0) + jnp.where(at == 36 + t, wide, 0.0),
                axis=1,
                keepdims=True,
            )
        )
    positive = jnp.where(left, halves[0], halves[1])
    peers(
        lambda n: copy_to(
            sc_send, sc_all.at[n], sc_ssem.at[n], sc_rsem.at[n], (rep, neg)
        ).wait()
    )

    def by_half(values):
        first = jnp.sum(jnp.where(left, values, 0.0), axis=1, keepdims=True)
        second = jnp.sum(jnp.where(left, 0.0, values), axis=1, keepdims=True)
        return jnp.where(left, first, second)

    all_scores = sc_all[...]
    shape = (NEGS, 32, 128)
    cand_id = (iota(shape, 0) * OWN + iota(shape, 2) % OWN).astype(F32)
    is_pos = cand_id == positive[None]
    pos_score = by_half(jnp.sum(jnp.where(is_pos, all_scores, 0.0), axis=0))
    gaps = all_scores - pos_score[None] + MARGIN
    small = jnp.exp(-jnp.abs(gaps))
    losses = jnp.maximum(gaps, 0.0) + jnp.log1p(small)
    sigmoid = jnp.where(gaps >= 0.0, 1.0, small) / (1.0 + small)
    loss = by_half(jnp.sum(losses, axis=0)) / (NEGS * OWN)
    totals = by_half(jnp.sum(sigmoid, axis=0))
    own_gap = sc_all[neg] - pos_score + MARGIN
    own_small = jnp.exp(-jnp.abs(own_gap))
    own_sig = jnp.where(own_gap >= 0.0, 1.0, own_small) / (1.0 + own_small)
    own_id = (neg * OWN + iota((32, 128), 1) % OWN).astype(F32)
    score_grad = (own_sig - jnp.where(own_id == positive, totals, 0.0)) / (NEGS * OWN)
    lines = (iota((8, 32), 1) == iota((8, 32), 0) + B * (neg % 8)).astype(F32)
    half = jnp.where(neg // 8 == 0, 0, OWN)
    mine = nn(lines, loss, HIGH)
    loss_ref[...] = jnp.sum(
        jnp.where(iota((8, 128), 1) == half, mine, 0.0), axis=1, keepdims=True
    ) + jnp.zeros((8, 128), F32)

    g_left = jnp.where(left, score_grad, 0.0).astype(BF16)
    g_right = jnp.where(left, 0.0, score_grad).astype(BF16)
    eg = jnp.concatenate([nn(g_left, cand_v[...]), nn(g_right, cand_v[...])], axis=0).astype(BF16)
    row_p, col_p = iota((256, 64), 0), iota((256, 64), 1)
    eg_out = jnp.zeros((256, part), F32)
    for c in range(4):
        move = bf((row_p // 16 == col_p // 4) & (row_p % 16 == 4 * c + col_p % 4))
        eg_out = eg_out + nn(move, eg[:, c * part : (c + 1) * part])
    eg_send[...] = eg_out.astype(BF16).reshape(NEGS, 16, part)
    peers(
        lambda n: copy_to(
            eg_send.at[n], eg_recv.at[neg], eg_ssem.at[n], eg_rsem.at[neg], (rep, n)
        ).start()
    )
    eg_recv[neg] = eg_send[neg]
    cand_out[...] = tn(g_left, e_v[0:32, :])[0:OWN] + tn(g_right, e_v[32:64, :])[OWN:128]
    peers(
        lambda n: copy_to(
            eg_send.at[n], eg_recv.at[n], eg_ssem.at[n], eg_rsem.at[n], (rep, neg)
        ).wait()
    )
    eg_sum = jnp.sum(eg_recv[...].astype(F32), axis=0)
    embed_grad = []
    for c in range(4):
        move = (
            (iota((8, 16), 1) == iota((8, 16), 0) + 4 * c) & (iota((8, 16), 0) < B)
        ).astype(F32)
        embed_grad.append(nn(move, eg_sum, HIGH))
    embed_grad = jnp.concatenate(embed_grad, axis=1)

    top_grad = inv_top * embed_grad - top_in * (
        inv_top * inv_top * inv_top * jnp.mean(embed_grad * top_in, axis=1, keepdims=True)
    )
    normed_grad = tn(hop_mat, top_grad, HIGH)
    mixed_grad = inv_mid * normed_grad - mixed * (
        inv_mid * inv_mid * inv_mid * jnp.mean(normed_grad * mixed, axis=1, keepdims=True)
    )
    mixed_in_grad = jnp.where(mixed_in > 0.0, mixed_grad, 0.0).astype(BF16)
    total = jnp.zeros((HOP1, H), F32)
    for j in range(TILES):
        total = total + nt(mixed_in_grad[:, j * TILE : (j + 1) * TILE], cw_v[j, F : F + H, :])
    pooled_g[...] = total

    other = (y * CORES + 1 - core, neg)
    for j in range(TILES):
        spread_grad = jnp.broadcast_to(
            pooled_g[:, j * TILE : (j + 1) * TILE][:, None, :], (HOP1, SLOTS, TILE)
        ).reshape(REQ, TILE)
        pgrad_v[...] = jnp.where(mask_v[j].astype(F32) > 0.0, spread_grad * weight, 0.0).astype(
            BF16
        )
        p_send[j] = nn(curt_v[1 - core], pgrad_v[...]).astype(BF16)
        copy_to(p_send.at[j], p_recv.at[j], p_ssem.at[j], p_rsem.at[j], other).start()
        p_own[j] = nn(curt_v[core], pgrad_v[...])

    half_tiles = TILES // 2

    def y_peers(body):
        def step(i, carry):
            body(lax.rem(y + i, YS))
            return carry

        lax.fori_loop(1, YS, step, 0)

    for j in range(TILES):
        copy_to(p_send.at[j], p_recv.at[j], p_ssem.at[j], p_rsem.at[j], other).wait()
        chip_sum = p_own[j] + p_recv[j].astype(F32)
        if j < half_tiles:
            a1_send[j] = chip_sum.astype(BF16).reshape(YS, 128, TILE)
            y_peers(
                lambda q, j=j: copy_to(
                    a1_send.at[j, q], a1_recv.at[j, y], a1_ssem.at[j, q], a1_rsem.at[j, y],
                    (q * CORES + core, neg),
                ).start()
            )
            a1_recv[j, y] = a1_send[j, y]
        else:
            k = j - half_tiles
            for q in range(YS):
                b1_f[:, 8 * q : 8 * q + 8, :] = chip_sum[128 * q : 128 * q + 128].reshape(
                    NEGS, 8, TILE
                )
            b1_send[k] = b1_f[...].astype(BF16)
            peers(
                lambda n, k=k: copy_to(
                    b1_send.at[k, n], b1_recv.at[k, neg], b1_ssem.at[k, n], b1_rsem.at[k, neg],
                    (rep, n),
                ).start()
            )
            b1_recv[k, neg] = b1_send[k, neg]

    for j in range(half_tiles):
        y_peers(
            lambda q, j=j: copy_to(
                a1_send.at[j, q], a1_recv.at[j, q], a1_ssem.at[j, q], a1_rsem.at[j, q],
                (rep, neg),
            ).wait()
        )
        a2_f[:, 8 * j : 8 * j + 8, :] = jnp.sum(a1_recv[j].astype(F32), axis=0).reshape(
            NEGS, 8, TILE
        )
    a2_send[...] = a2_f[...].astype(BF16)
    peers(
        lambda n: copy_to(
            a2_send.at[n], a2_recv.at[neg], a2_ssem.at[n], a2_rsem.at[neg], (rep, n)
        ).start()
    )
    a2_recv[neg] = a2_send[neg]
    for k in range(half_tiles):
        peers(
            lambda n, k=k: copy_to(
                b1_send.at[k, n], b1_recv.at[k, n], b1_ssem.at[k, n], b1_rsem.at[k, n],
                (rep, neg),
            ).wait()
        )
        b2_f[:, 8 * k : 8 * k + 8, :] = jnp.sum(b1_recv[k].astype(F32), axis=0).reshape(
            YS, 8, TILE
        )
    b2_send[...] = b2_f[...].astype(BF16)
    y_peers(
        lambda q: copy_to(
            b2_send.at[q], b2_recv.at[y], b2_ssem.at[q], b2_rsem.at[y], (q * CORES + core, neg)
        ).start()
    )
    b2_recv[y] = b2_send[y]

    owner_col = cols_v[:, 0:1]
    rank_col = cols_v[:, 1:2]
    third = jnp.floor((rank_col + 0.5) * (1.0 / 3.0))
    left_over = rank_col - 3.0 * third
    slot_main = owner_col * 16.0 + rank_col
    slot_tail = owner_col * 16.0 + 12.0 + third

    def place(step, carry):
        g = lax.rem(rep - step + REPS, REPS)

        def arrive(i, carry):
            d = g * NEGS + lax.rem(neg + i, NEGS)

            @pl.when(d != me)
            def _():
                copy_to(
                    row_send.at[d], row_recv.at[d], row_ssem.at[d], row_rsem.at[d], (rep, neg)
                ).wait()

            return carry

        lax.fori_loop(0, NEGS, arrive, 0)
        block = row_recv[pl.ds(pl.multiple_of(g * NEGS, NEGS), NEGS)].reshape(256, WIDE)
        line = (iota((REQ, 256), 1) + g * 256).astype(F32)
        new = [nn(bf(line == slot_main), block)]
        tail = jnp.zeros((REQ, TILE), F32)
        for c in range(3):
            pick = bf((line == slot_tail) & (left_over == float(c)))
            tail = tail + nn(pick, block[:, c * TILE : (c + 1) * TILE])
        new = jnp.concatenate(new + [tail], axis=1).astype(BF16)

        @pl.when(step == 0)
        def _():
            rows_acc[...] = new

        @pl.when(step > 0)
        def _():
            rows_acc[...] = rows_acc[...] + new

        return carry

    lax.fori_loop(0, REPS, place, 0)
    out = pltpu.make_async_copy(rows_acc, rows_hbm, out_sem)
    out.start()

    peers(
        lambda n: copy_to(
            a2_send.at[n], a2_recv.at[n], a2_ssem.at[n], a2_rsem.at[n], (rep, neg)
        ).wait()
    )
    y_peers(
        lambda q: copy_to(
            b2_send.at[q], b2_recv.at[q], b2_ssem.at[q], b2_rsem.at[q], (rep, neg)
        ).wait()
    )
    a_sum = jnp.sum(a2_recv[...].astype(F32), axis=0)
    b_sum = jnp.sum(b2_recv[...].astype(F32), axis=0)
    for j in range(half_tiles):
        ngrad_ref[:, j * TILE : (j + 1) * TILE] = a_sum[8 * j : 8 * j + 8]
        ngrad_ref[:, (j + half_tiles) * TILE : (j + half_tiles + 1) * TILE] = b_sum[
            8 * j : 8 * j + 8
        ]
    out.wait()


def local(
    feature_table, cur_rows, next_owner, next_local, slot_counts, hop_counts, positive_ids,
    neighbor_weight, combine_weight, candidates,
):
    vmem = pl.BlockSpec(memory_space=pltpu.VMEM)
    smem = pl.BlockSpec(memory_space=pltpu.SMEM)
    hbm = pl.BlockSpec(memory_space=pl.ANY)
    dma = pltpu.SemaphoreType.DMA
    part = H // 4
    scratch = [
        pltpu.VMEM((REQ, F), BF16),
        pltpu.VMEM((2, 512, REQ), BF16),
        pltpu.VMEM((F, F), BF16),
        pltpu.VMEM((TILES, F, TILE), BF16),
        pltpu.VMEM((TILES, F + H, TILE), BF16),
        pltpu.VMEM((2 * OWN, H), BF16),
        pltpu.VMEM((TILES, REQ, TILE), BF16),
        pltpu.VMEM((REQ, TILE), BF16),
        pltpu.VMEM((HOP1, F + H), BF16),
        pltpu.VMEM((HOP1, H), F32),
        pltpu.VMEM((HOP1, H), F32),
        pltpu.VMEM((DEVS, 1, 128), F32),
        pltpu.VMEM((DEVS, 1, 128), F32),
        pltpu.VMEM((DEVS, 128), F32),
        pltpu.VMEM((DEVS, 16, WIDE), BF16),
        pltpu.VMEM((DEVS, 16, WIDE), BF16),
        pltpu.VMEM((REQ, F), BF16),
        pltpu.VMEM((REQ, 16), F32),
        pltpu.VMEM((16, part), BF16),
        pltpu.VMEM((NEGS, 16, part), BF16),
        pltpu.VMEM((64, H), BF16),
        pltpu.VMEM((32, 128), F32),
        pltpu.VMEM((NEGS, 32, 128), F32),
        pltpu.VMEM((NEGS, 16, part), BF16),
        pltpu.VMEM((NEGS, 16, part), BF16),
        pltpu.VMEM((TILES, 512, TILE), BF16),
        pltpu.VMEM((TILES, 512, TILE), BF16),
        pltpu.VMEM((TILES, 512, TILE), F32),
        pltpu.VMEM((4, YS, 128, TILE), BF16),
        pltpu.VMEM((4, YS, 128, TILE), BF16),
        pltpu.VMEM((NEGS, 32, TILE), F32),
        pltpu.VMEM((NEGS, 32, TILE), BF16),
        pltpu.VMEM((NEGS, 32, TILE), BF16),
        pltpu.VMEM((NEGS, 32, TILE), F32),
        pltpu.VMEM((4, NEGS, 32, TILE), BF16),
        pltpu.VMEM((4, NEGS, 32, TILE), BF16),
        pltpu.VMEM((YS, 32, TILE), F32),
        pltpu.VMEM((YS, 32, TILE), BF16),
        pltpu.VMEM((YS, 32, TILE), BF16),
        dma((20,)), dma(()),
        dma((DEVS,)), dma((DEVS,)), dma((DEVS,)), dma((DEVS,)),
        dma((NEGS,)), dma((NEGS,)), dma((NEGS,)), dma((NEGS,)), dma((NEGS,)), dma((NEGS,)),
        dma((TILES,)), dma((TILES,)),
        dma((4, YS)), dma((4, YS)),
        dma((NEGS,)), dma((NEGS,)),
        dma((4, NEGS)), dma((4, NEGS)),
        dma((YS,)), dma((YS,)),
    ]
    next_rows, loss, cand_grad, neighbor_grad = pl.pallas_call(
        kernel,
        out_shape=(
            jax.ShapeDtypeStruct((REQ, F), BF16),
            jax.ShapeDtypeStruct((8, 128), F32),
            jax.ShapeDtypeStruct((OWN, H), F32),
            jax.ShapeDtypeStruct((8, H), F32),
        ),
        in_specs=[vmem, vmem, vmem, vmem, smem, hbm, hbm, hbm, hbm, hbm],
        out_specs=(hbm, vmem, vmem, vmem),
        scratch_shapes=scratch,
        compiler_params=pltpu.CompilerParams(
            collective_id=0, has_side_effects=True, vmem_limit_bytes=62 * 2**20
        ),
        name="step",
    )(
        next_owner.reshape(1, REQ),
        next_local.reshape(1, REQ),
        slot_counts.T,
        hop_counts,
        positive_ids.reshape(1, B),
        feature_table,
        cur_rows,
        neighbor_weight,
        combine_weight,
        candidates,
    )
    return next_rows, loss[:B, 0], cand_grad, neighbor_grad


def solution(mesh):
    both = P(("rep", "neg"), None)
    flat = P(("rep", "neg"))
    return jax.shard_map(
        local,
        mesh=mesh,
        in_specs=(both, both, both, flat, both, both, flat, P(), P(), both),
        out_specs=(both, flat, both, both),
        check_vma=False,
    )
```

```python
import jax
import jax.numpy as jnp
from jax import lax
from jax.experimental import pallas as pl
from jax.experimental.pallas import tpu as pltpu
from jax.sharding import PartitionSpec as P

EPSILON = 1e-06
MARGIN = 0.5
MESH = pl.DeviceIdType.MESH
F32 = jnp.float32
BF16 = jnp.bfloat16
HIGH = lax.Precision.HIGHEST

REPS, NEGS, DEVS = 8, 16, 128
YS, CORES = 4, 2
F, H = 1024, 2048
TILE = 512
TILES = H // TILE
REQ, HOP1, SLOTS, B, K1 = 768, 48, 16, 4, 12
PART = 256
WIDE = 3 * PART
OWN = 64


def iota(shape, dim):
    return lax.broadcasted_iota(jnp.int32, shape, dim)


def nt(a, b, precision=None):
    return lax.dot_general(
        a, b, (((1,), (1,)), ((), ())), preferred_element_type=F32, precision=precision
    )


def tn(a, b, precision=None):
    return lax.dot_general(
        a, b, (((0,), (0,)), ((), ())), preferred_element_type=F32, precision=precision
    )


def nn(a, b, precision=None):
    return jnp.dot(a, b, preferred_element_type=F32, precision=precision)


def bf(mask):
    return mask.astype(F32).astype(BF16)


def kernel(
    owner_ref, local_ref, slot_ref, hop_ref, pos_ref,
    table_hbm, cur_hbm, nw_hbm, cw_hbm, cand_hbm,
    rows_hbm, loss_ref, cand_out, ngrad_ref,
    cur_v, curt_v, table_v, nw_v, cw_v, cand_v, mask_v, pgrad_v, x_v, mixed_v, pooled_g,
    ask_send, ask_mid, ask_recv, ids_v, row_out, row_send, row_recv, rows_acc, cols_v,
    emb_send, emb_all, e_v, sc_send, sc_all, eg_send, eg_recv,
    p_send, p_recv, p_own, a1_send, a1_recv, a2_f, a2_send, a2_recv,
    b1_f, b1_send, b1_recv, b2_f, b2_send, b2_recv,
    in_sem, out_sem, ask_sem, out_ssem, out_rsem, row_ssem, row_rsem,
    emb_sem, sc_sem, eg_sem, p_ssem, p_rsem, a1_ssem, a1_rsem, a2_sem, b1_ssem, b1_rsem, b2_sem,
):
    rep = lax.axis_index("rep")
    neg = lax.axis_index("neg")
    y, core = rep // CORES, rep % CORES
    mate = (y * CORES + 1 - core, neg)

    def send(src, dst, ssem, rsem, where):
        pltpu.make_async_remote_copy(
            src_ref=src, dst_ref=dst, send_sem=ssem, recv_sem=rsem,
            device_id=where, device_id_type=MESH,
        ).start()

    def settle(ref, sem):
        pltpu.make_async_copy(ref, ref, sem).wait()

    def around(here, count, body):
        def step(i, carry):
            body(lax.rem(here + i, count))
            return carry

        lax.fori_loop(1, count, step, 0)

    loads = [
        pltpu.make_async_copy(cur_hbm, cur_v, in_sem.at[0]),
        pltpu.make_async_copy(table_hbm, table_v, in_sem.at[1]),
        pltpu.make_async_copy(cand_hbm, cand_v.at[pl.ds(0, OWN)], in_sem.at[2]),
        pltpu.make_async_copy(cand_hbm, cand_v.at[pl.ds(OWN, OWN)], in_sem.at[3]),
    ]
    nw_loads = [
        pltpu.make_async_copy(
            nw_hbm.at[:, pl.ds(j * TILE, TILE)], nw_v.at[j], in_sem.at[4 + j]
        )
        for j in range(TILES)
    ]
    cw_loads = [
        pltpu.make_async_copy(
            cw_hbm.at[:, pl.ds(j * TILE, TILE)], cw_v.at[j], in_sem.at[4 + TILES + j]
        )
        for j in range(TILES)
    ]
    loads[0].start()
    for load in nw_loads:
        load.start()
    for load in loads[1:]:
        load.start()
    for load in cw_loads:
        load.start()

    barrier = pltpu.get_barrier_semaphore()

    def greet(where):
        pl.semaphore_signal(barrier, inc=1, device_id=where, device_id_type=MESH)

    around(neg, NEGS, lambda n: greet((rep, n)))
    around(rep, REPS, lambda r: greet((r, neg)))

    owner = owner_ref[...]
    hit = owner == iota((DEVS, REQ), 0)
    hit_low = bf(hit)
    before = bf(iota((REQ, REQ), 0) < iota((REQ, REQ), 1))
    count = nn(hit_low, before)
    rank = jnp.sum(jnp.where(hit, count, 0.0), axis=0, keepdims=True)
    local = local_ref[...].reshape(1, REQ)
    line = iota((DEVS, REQ), 0).astype(F32)
    pay = jnp.where(line == rank, (local >> 5).astype(F32), 0.0) + jnp.where(
        line == rank + 16.0, (local & 31).astype(F32), 0.0
    )
    asks = nt(hit_low, pay.astype(BF16))
    lane1 = iota((1, 128), 1)
    positives = jnp.zeros((1, 128), jnp.int32)
    for t in range(B):
        value = pos_ref[t]
        positives = positives + jnp.where(lane1 == 32 + t, value >> 5, 0)
        positives = positives + jnp.where(lane1 == 36 + t, value & 31, 0)
    asks = asks + positives.astype(F32)
    ask_send[...] = asks.reshape(REPS, NEGS, 1, 128)

    pl.semaphore_wait(barrier, NEGS - 1 + REPS - 1)
    around(
        rep, REPS,
        lambda r: send(
            ask_send.at[r], ask_mid.at[rep], ask_sem.at[0], ask_sem.at[1], (r, neg)
        ),
    )
    ask_mid[rep] = ask_send[rep]

    placed = (owner >> 5) * 32 + (owner & 15) * 2 + ((owner >> 4) & 1)
    eye = bf(iota((REQ, REQ), 0) == iota((REQ, REQ), 1))
    pair = jnp.where(iota((16, REQ), 0) == 0, placed.astype(F32), rank).astype(BF16)
    cols_v[...] = nt(eye, pair)

    spread = bf(iota((REQ, HOP1), 0) // SLOTS == iota((REQ, HOP1), 1))
    counts = nt(spread, slot_ref[...].astype(F32).astype(BF16))
    at_slot = iota((REQ, SLOTS), 0) % SLOTS == iota((REQ, SLOTS), 1)
    weight = jnp.sum(jnp.where(at_slot, counts, 0.0), axis=1, keepdims=True) / jnp.sum(
        counts, axis=1, keepdims=True
    )

    loads[0].wait()

    def project(j):
        nw_loads[j].wait()
        projected = nn(cur_v[...], nw_v[j])
        mask_v[j] = bf(projected > 0.0)
        weighted = jnp.maximum(projected, 0.0) * weight
        pooled = jnp.sum(weighted.reshape(HOP1, SLOTS, TILE), axis=1)
        x_v[:, F + j * TILE : F + (j + 1) * TILE] = pooled.astype(BF16)

    for j in range(TILES // 2):
        project(j)
    settle(ask_mid.at[pl.ds(0, REPS - 1)], ask_sem.at[1])
    around(
        neg, NEGS,
        lambda n: send(
            ask_mid.at[:, n], ask_recv.at[:, neg], ask_sem.at[2], ask_sem.at[3], (rep, n)
        ),
    )
    ask_recv[:, neg] = ask_mid[:, neg]
    for j in range(TILES // 2, TILES):
        project(j)
    first = bf(iota((HOP1, REQ), 0) * SLOTS == iota((HOP1, REQ), 1))
    x_v[:, 0:F] = nn(first, cur_v[...]).astype(BF16)
    loads[1].wait()
    settle(ask_recv.at[:, pl.ds(0, NEGS - 1)], ask_sem.at[3])
    ids_v[...] = ask_recv[...].reshape(DEVS, 128)

    def serve(g):
        base = pl.multiple_of(g * NEGS, NEGS)
        asked = ids_v[pl.ds(base, NEGS), :].astype(BF16)

        def chosen(rows, per, slot_of):
            wide = nn(bf(iota((rows, NEGS), 0) // per % NEGS == iota((rows, NEGS), 1)), asked)
            slot = slot_of(iota((rows, 1), 0))
            at = iota((rows, 128), 1)
            ids = jnp.sum(
                jnp.where(at == slot, wide * 32.0, 0.0) + jnp.where(at == slot + 16, wide, 0.0),
                axis=1,
                keepdims=True,
            )
            return bf(ids == iota((rows, F), 1).astype(F32))

        main = nn(chosen(256, 16, lambda r: r % 16), table_v[:, 0:WIDE]).reshape(NEGS, 16, WIDE)
        tail = nn(
            chosen(384, 8, lambda r: jnp.maximum(r % 8 - 4, 0) * 3 + r // 128),
            table_v[:, WIDE:F],
        )
        high = iota((NEGS, 8, PART), 1) >= 4
        parts = []
        for c in range(3):
            own = main[:, 8:16, c * PART : (c + 1) * PART]
            parts.append(
                jnp.where(high, tail[128 * c : 128 * (c + 1)].reshape(NEGS, 8, PART), own)
            )
        lower = jnp.concatenate(parts, axis=2)
        return jnp.concatenate([main[:, 0:8, :], lower], axis=1).astype(BF16)

    def round_of(k):
        to_y = lax.rem(y + k, YS)
        row_out[k] = serve(to_y * CORES + 1 - core)
        send(row_out.at[k], row_send.at[to_y, :, core], out_ssem.at[k], out_rsem.at[k], mate)
        row_send[to_y, :, core] = serve(to_y * CORES + core)
        settle(row_out.at[k], out_rsem.at[k])

        def post(n):
            send(
                row_send.at[to_y, n], row_recv.at[y, neg], row_ssem.at[k], row_rsem.at[y],
                (to_y * CORES + core, n),
            )

        around(neg, NEGS, post)
        if k == 0:
            row_recv[y, neg] = row_send[y, neg]
        else:
            post(neg)

    round_of(0)

    x = x_v[...]
    for j in range(TILES):
        cw_loads[j].wait()
        mixed_v[:, j * TILE : (j + 1) * TILE] = nn(x, cw_v[j])
    mixed_in = mixed_v[...]
    mixed = jnp.maximum(mixed_in, 0.0)
    inv_mid = lax.rsqrt(jnp.mean(mixed * mixed, axis=1, keepdims=True) + EPSILON)
    normed = mixed * inv_mid
    top_rows = bf(iota((8, B), 0) == iota((8, B), 1))
    hops = nn(top_rows, hop_ref[...].astype(F32).astype(BF16))
    lanes_of = bf(iota((K1, HOP1), 0) == iota((K1, HOP1), 1) % K1)
    own_hop = iota((8, HOP1), 0) == iota((8, HOP1), 1) // K1
    hop_total = jnp.maximum(jnp.sum(hops, axis=1, keepdims=True), 1.0)
    hop_mat = jnp.where(own_hop, nn(hops.astype(BF16), lanes_of), 0.0) / hop_total
    top_in = nn(hop_mat, normed, HIGH)
    inv_top = lax.rsqrt(jnp.mean(top_in * top_in, axis=1, keepdims=True) + EPSILON)
    embedding = (top_in * inv_top).astype(BF16)
    part = H // 4
    packed = jnp.zeros((16, part), F32)
    for c in range(4):
        move = bf(
            (iota((16, 8), 0) == iota((16, 8), 1) + 4 * c) & (iota((16, 8), 1) < B)
        )
        packed = packed + nn(move, embedding[:, c * part : (c + 1) * part])
    emb_send[...] = packed.astype(BF16)
    around(
        neg, NEGS,
        lambda n: send(emb_send, emb_all.at[neg], emb_sem.at[0], emb_sem.at[1], (rep, n)),
    )
    emb_all[neg] = emb_send[...]

    round_of(1)

    loads[2].wait()
    loads[3].wait()
    settle(emb_all.at[pl.ds(0, NEGS - 1)], emb_sem.at[1])

    gathered = emb_all[...].reshape(256, part)
    row_q, col_q = iota((64, 256), 0), iota((64, 256), 1)
    for c in range(4):
        move = bf(col_q == (row_q // 4) * 16 + 4 * c + row_q % 4)
        e_v[:, c * part : (c + 1) * part] = nn(move, gathered).astype(BF16)
    left = iota((32, 128), 1) < OWN
    scores = jnp.where(left, nt(e_v[0:32, :], cand_v[...]), nt(e_v[32:64, :], cand_v[...]))
    sc_send[...] = scores
    around(
        neg, NEGS,
        lambda n: send(sc_send, sc_all.at[neg], sc_sem.at[0], sc_sem.at[1], (rep, n)),
    )
    sc_all[neg] = scores

    round_of(2)

    mates = ids_v[pl.ds(pl.multiple_of(rep * NEGS, NEGS), NEGS), :].astype(BF16)
    halves = []
    for h in range(2):
        pick = bf(iota((32, NEGS), 0) // B + 8 * h == iota((32, NEGS), 1))
        wide = nn(pick, mates)
        at, t = iota((32, 128), 1), iota((32, 128), 0) % B
        halves.append(
            jnp.sum(
                jnp.where(at == 32 + t, wide * 32.0, 0.0) + jnp.where(at == 36 + t, wide, 0.0),
                axis=1,
                keepdims=True,
            )
        )
    positive = jnp.where(left, halves[0], halves[1])
    settle(sc_all.at[pl.ds(0, NEGS - 1)], sc_sem.at[1])

    def by_half(values):
        first = jnp.sum(jnp.where(left, values, 0.0), axis=1, keepdims=True)
        second = jnp.sum(jnp.where(left, 0.0, values), axis=1, keepdims=True)
        return jnp.where(left, first, second)

    all_scores = sc_all[...]
    shape = (NEGS, 32, 128)
    cand_id = (iota(shape, 0) * OWN + iota(shape, 2) % OWN).astype(F32)
    is_pos = cand_id == positive[None]
    pos_score = by_half(jnp.sum(jnp.where(is_pos, all_scores, 0.0), axis=0))
    gaps = all_scores - pos_score[None] + MARGIN
    small = jnp.exp(-jnp.abs(gaps))
    losses = jnp.maximum(gaps, 0.0) + jnp.log1p(small)
    sigmoid = jnp.where(gaps >= 0.0, 1.0, small) / (1.0 + small)
    loss = by_half(jnp.sum(losses, axis=0)) / (NEGS * OWN)
    totals = by_half(jnp.sum(sigmoid, axis=0))
    own_gap = sc_all[neg] - pos_score + MARGIN
    own_small = jnp.exp(-jnp.abs(own_gap))
    own_sig = jnp.where(own_gap >= 0.0, 1.0, own_small) / (1.0 + own_small)
    own_id = (neg * OWN + iota((32, 128), 1) % OWN).astype(F32)
    score_grad = (own_sig - jnp.where(own_id == positive, totals, 0.0)) / (NEGS * OWN)

    g_left = jnp.where(left, score_grad, 0.0).astype(BF16)
    g_right = jnp.where(left, 0.0, score_grad).astype(BF16)
    eg = jnp.concatenate([nn(g_left, cand_v[...]), nn(g_right, cand_v[...])], axis=0).astype(BF16)
    row_p, col_p = iota((256, 64), 0), iota((256, 64), 1)
    eg_out = jnp.zeros((256, part), F32)
    for c in range(4):
        move = bf((row_p // 16 == col_p // 4) & (row_p % 16 == 4 * c + col_p % 4))
        eg_out = eg_out + nn(move, eg[:, c * part : (c + 1) * part])
    eg_send[...] = eg_out.astype(BF16).reshape(NEGS, 16, part)
    around(
        neg, NEGS,
        lambda n: send(eg_send.at[n], eg_recv.at[neg], eg_sem.at[0], eg_sem.at[1], (rep, n)),
    )
    eg_recv[neg] = eg_send[neg]

    round_of(3)

    lines = (iota((32, 128), 0) == iota((32, 128), 1) + B * (neg % 8)).astype(F32)
    half = jnp.where(neg // 8 == 0, 0, OWN)
    mine = tn(loss, lines, HIGH)
    loss_ref[...] = jnp.sum(
        jnp.where(iota((128, 128), 0) == half, mine, 0.0), axis=0, keepdims=True
    )[:, 0:B]
    cand_out[...] = tn(g_left, e_v[0:32, :])[0:OWN] + tn(g_right, e_v[32:64, :])[OWN:128]
    for b in range(8):
        curt_v[b % 2, 128 * (b // 2) : 128 * (b // 2) + 128, :] = (
            cur_v[:, 128 * b : 128 * b + 128].astype(F32).T.astype(BF16)
        )
    settle(eg_recv.at[pl.ds(0, NEGS - 1)], eg_sem.at[1])
    eg_sum = jnp.sum(eg_recv[...].astype(F32), axis=0)
    embed_grad = []
    for c in range(4):
        move = (
            (iota((8, 16), 1) == iota((8, 16), 0) + 4 * c) & (iota((8, 16), 0) < B)
        ).astype(F32)
        embed_grad.append(nn(move, eg_sum, HIGH))
    embed_grad = jnp.concatenate(embed_grad, axis=1)

    top_grad = inv_top * embed_grad - top_in * (
        inv_top * inv_top * inv_top * jnp.mean(embed_grad * top_in, axis=1, keepdims=True)
    )
    normed_grad = tn(hop_mat, top_grad, HIGH)
    mixed_grad = inv_mid * normed_grad - mixed * (
        inv_mid * inv_mid * inv_mid * jnp.mean(normed_grad * mixed, axis=1, keepdims=True)
    )
    mixed_in_grad = jnp.where(mixed_in > 0.0, mixed_grad, 0.0).astype(BF16)
    total = jnp.zeros((HOP1, H), F32)
    for j in range(TILES):
        total = total + nt(mixed_in_grad[:, j * TILE : (j + 1) * TILE], cw_v[j, F : F + H, :])
    pooled_g[...] = total

    order = (0, 2, 1, 3)
    for j in order:
        spread_grad = jnp.broadcast_to(
            pooled_g[:, j * TILE : (j + 1) * TILE][:, None, :], (HOP1, SLOTS, TILE)
        ).reshape(REQ, TILE)
        pgrad_v[...] = jnp.where(mask_v[j].astype(F32) > 0.0, spread_grad * weight, 0.0).astype(
            BF16
        )
        p_send[j] = nn(curt_v[1 - core], pgrad_v[...]).astype(BF16)
        send(p_send.at[j], p_recv.at[j], p_ssem.at[j], p_rsem.at[j], mate)
        p_own[j] = nn(curt_v[core], pgrad_v[...])

    for j in order:
        settle(p_recv.at[j], p_rsem.at[j])
        chip_sum = p_own[j] + p_recv[j].astype(F32)
        if j < 2:
            a1_send[j] = chip_sum.astype(BF16).reshape(YS, 128, TILE)
            around(
                y, YS,
                lambda q, j=j: send(
                    a1_send.at[j, q], a1_recv.at[j, y], a1_ssem.at[j], a1_rsem.at[j],
                    (q * CORES + core, neg),
                ),
            )
            a1_recv[j, y] = a1_send[j, y]
        else:
            k = j - 2
            for q in range(YS):
                b1_f[:, 8 * q : 8 * q + 8, :] = chip_sum[128 * q : 128 * q + 128].reshape(
                    NEGS, 8, TILE
                )
            b1_send[k] = b1_f[...].astype(BF16)
            around(
                neg, NEGS,
                lambda n, k=k: send(
                    b1_send.at[k, n], b1_recv.at[k, neg], b1_ssem.at[k], b1_rsem.at[k], (rep, n)
                ),
            )
            b1_recv[k, neg] = b1_send[k, neg]

    owner_col = cols_v[:, 0:1]
    rank_col = cols_v[:, 1:2]
    third = jnp.floor((rank_col + 0.5) * (1.0 / 3.0))
    left_over = rank_col - 3.0 * third
    slot_main = owner_col * 16.0 + rank_col
    slot_tail = [
        jnp.where(left_over == float(c), owner_col * 16.0 + 12.0 + third, -1.0) for c in range(3)
    ]

    def place(k):
        from_y = lax.rem(y - k + YS, YS)
        got = NEGS - 1 if k == 0 else NEGS
        settle(row_recv.at[from_y, pl.ds(0, got)], row_rsem.at[from_y])
        block = row_recv[from_y].reshape(512, WIDE)
        line = (iota((REQ, 512), 1) + from_y * 512).astype(F32)
        body = nn(bf(line == slot_main), block)
        tail = jnp.zeros((REQ, PART), F32)
        for c in range(3):
            tail = tail + nn(bf(line == slot_tail[c]), block[:, c * PART : (c + 1) * PART])
        new = jnp.concatenate([body, tail], axis=1).astype(BF16)
        rows_acc[...] = new if k == 0 else rows_acc[...] + new

    place(0)
    place(1)

    for j in range(2):
        settle(a1_recv.at[j, pl.ds(0, YS - 1)], a1_rsem.at[j])
        a2_f[:, 8 * j : 8 * j + 8, :] = jnp.sum(a1_recv[j].astype(F32), axis=0).reshape(
            NEGS, 8, TILE
        )
    a2_send[...] = a2_f[...].astype(BF16)
    around(
        neg, NEGS,
        lambda n: send(a2_send.at[n], a2_recv.at[neg], a2_sem.at[0], a2_sem.at[1], (rep, n)),
    )
    a2_recv[neg] = a2_send[neg]
    for k in range(2):
        settle(b1_recv.at[k, pl.ds(0, NEGS - 1)], b1_rsem.at[k])
        b2_f[:, 8 * k : 8 * k + 8, :] = jnp.sum(b1_recv[k].astype(F32), axis=0).reshape(
            YS, 8, TILE
        )
    b2_send[...] = b2_f[...].astype(BF16)
    around(
        y, YS,
        lambda q: send(
            b2_send.at[q], b2_recv.at[y], b2_sem.at[0], b2_sem.at[1], (q * CORES + core, neg)
        ),
    )
    b2_recv[y] = b2_send[y]

    place(2)
    place(3)
    out = pltpu.make_async_copy(rows_acc, rows_hbm, out_sem)
    out.start()

    settle(a2_recv.at[pl.ds(0, NEGS - 1)], a2_sem.at[1])
    a_sum = jnp.sum(a2_recv[...].astype(F32), axis=0)
    settle(b2_recv.at[pl.ds(0, YS - 1)], b2_sem.at[1])
    b_sum = jnp.sum(b2_recv[...].astype(F32), axis=0)
    for j in range(2):
        ngrad_ref[:, j * TILE : (j + 1) * TILE] = a_sum[8 * j : 8 * j + 8]
        ngrad_ref[:, (j + 2) * TILE : (j + 3) * TILE] = b_sum[8 * j : 8 * j + 8]

    settle(ask_send.at[pl.ds(0, REPS - 1)], ask_sem.at[0])
    settle(ask_mid.at[:, pl.ds(0, NEGS - 1)], ask_sem.at[2])
    for k in range(YS):
        settle(row_out.at[k], out_ssem.at[k])
        settle(row_send.at[k, pl.ds(0, NEGS - 1 if k == 0 else NEGS)], row_ssem.at[k])
    settle(emb_all.at[pl.ds(0, NEGS - 1)], emb_sem.at[0])
    settle(sc_all.at[pl.ds(0, NEGS - 1)], sc_sem.at[0])
    settle(eg_send.at[pl.ds(0, NEGS - 1)], eg_sem.at[0])
    for j in range(TILES):
        settle(p_send.at[j], p_ssem.at[j])
    for j in range(2):
        settle(a1_send.at[j, pl.ds(0, YS - 1)], a1_ssem.at[j])
        settle(b1_send.at[j, pl.ds(0, NEGS - 1)], b1_ssem.at[j])
    settle(a2_send.at[pl.ds(0, NEGS - 1)], a2_sem.at[0])
    settle(b2_send.at[pl.ds(0, YS - 1)], b2_sem.at[0])
    out.wait()


def local(
    feature_table, cur_rows, next_owner, next_local, slot_counts, hop_counts, positive_ids,
    neighbor_weight, combine_weight, candidates,
):
    vmem = pl.BlockSpec(memory_space=pltpu.VMEM)
    smem = pl.BlockSpec(memory_space=pltpu.SMEM)
    hbm = pl.BlockSpec(memory_space=pl.ANY)
    dma = pltpu.SemaphoreType.DMA
    part = H // 4
    scratch = [
        pltpu.VMEM((REQ, F), BF16),
        pltpu.VMEM((2, 512, REQ), BF16),
        pltpu.VMEM((F, F), BF16),
        pltpu.VMEM((TILES, F, TILE), BF16),
        pltpu.VMEM((TILES, F + H, TILE), BF16),
        pltpu.VMEM((2 * OWN, H), BF16),
        pltpu.VMEM((TILES, REQ, TILE), BF16),
        pltpu.VMEM((REQ, TILE), BF16),
        pltpu.VMEM((HOP1, F + H), BF16),
        pltpu.VMEM((HOP1, H), F32),
        pltpu.VMEM((HOP1, H), F32),
        pltpu.VMEM((REPS, NEGS, 1, 128), F32),
        pltpu.VMEM((REPS, NEGS, 1, 128), F32),
        pltpu.VMEM((REPS, NEGS, 1, 128), F32),
        pltpu.VMEM((DEVS, 128), F32),
        pltpu.VMEM((YS, NEGS, 16, WIDE), BF16),
        pltpu.VMEM((YS, NEGS, CORES, 16, WIDE), BF16),
        pltpu.VMEM((YS, NEGS, CORES, 16, WIDE), BF16),
        pltpu.VMEM((REQ, F), BF16),
        pltpu.VMEM((REQ, 16), F32),
        pltpu.VMEM((16, part), BF16),
        pltpu.VMEM((NEGS, 16, part), BF16),
        pltpu.VMEM((64, H), BF16),
        pltpu.VMEM((32, 128), F32),
        pltpu.VMEM((NEGS, 32, 128), F32),
        pltpu.VMEM((NEGS, 16, part), BF16),
        pltpu.VMEM((NEGS, 16, part), BF16),
        pltpu.VMEM((TILES, 512, TILE), BF16),
        pltpu.VMEM((TILES, 512, TILE), BF16),
        pltpu.VMEM((TILES, 512, TILE), F32),
        pltpu.VMEM((2, YS, 128, TILE), BF16),
        pltpu.VMEM((2, YS, 128, TILE), BF16),
        pltpu.VMEM((NEGS, 16, TILE), F32),
        pltpu.VMEM((NEGS, 16, TILE), BF16),
        pltpu.VMEM((NEGS, 16, TILE), BF16),
        pltpu.VMEM((NEGS, 32, TILE), F32),
        pltpu.VMEM((2, NEGS, 32, TILE), BF16),
        pltpu.VMEM((2, NEGS, 32, TILE), BF16),
        pltpu.VMEM((YS, 16, TILE), F32),
        pltpu.VMEM((YS, 16, TILE), BF16),
        pltpu.VMEM((YS, 16, TILE), BF16),
        dma((4 + 2 * TILES,)), dma(()),
        dma((4,)), dma((YS,)), dma((YS,)), dma((YS,)), dma((YS,)),
        dma((2,)), dma((2,)), dma((2,)),
        dma((TILES,)), dma((TILES,)),
        dma((2,)), dma((2,)), dma((2,)),
        dma((2,)), dma((2,)), dma((2,)),
    ]
    next_rows, loss, cand_grad, neighbor_grad = pl.pallas_call(
        kernel,
        out_shape=(
            jax.ShapeDtypeStruct((REQ, F), BF16),
            jax.ShapeDtypeStruct((1, B), F32),
            jax.ShapeDtypeStruct((OWN, H), F32),
            jax.ShapeDtypeStruct((8, H), F32),
        ),
        in_specs=[vmem, vmem, vmem, vmem, smem, hbm, hbm, hbm, hbm, hbm],
        out_specs=(hbm, vmem, vmem, vmem),
        scratch_shapes=scratch,
        compiler_params=pltpu.CompilerParams(
            collective_id=0, has_side_effects=True, vmem_limit_bytes=62 * 2**20
        ),
        name="step",
    )(
        next_owner.reshape(1, REQ),
        next_local,
        slot_counts.T,
        hop_counts,
        positive_ids,
        feature_table,
        cur_rows,
        neighbor_weight,
        combine_weight,
        candidates,
    )
    return next_rows, loss.reshape(B), cand_grad, neighbor_grad


def solution(mesh):
    both = P(("rep", "neg"), None)
    flat = P(("rep", "neg"))
    return jax.shard_map(
        local,
        mesh=mesh,
        in_specs=(both, both, both, flat, both, both, flat, P(), P(), both),
        out_specs=(both, flat, both, both),
        check_vma=False,
    )
```

```python
import jax
import jax.numpy as jnp
from jax import lax
from jax.experimental import pallas as pl
from jax.experimental.pallas import tpu as pltpu
from jax.sharding import PartitionSpec as P

EPSILON = 1e-06
MARGIN = 0.5
MESH = pl.DeviceIdType.MESH
F32 = jnp.float32
BF16 = jnp.bfloat16
HIGH = lax.Precision.HIGHEST

REPS, NEGS, DEVS = 8, 16, 128
YS, CORES = 4, 2
F, H = 1024, 2048
TILE = 512
TILES = H // TILE
REQ, HOP1, SLOTS, B, K1 = 768, 48, 16, 4, 12
PART = 256
WIDE = 3 * PART
OWN = 64


def iota(shape, dim):
    return lax.broadcasted_iota(jnp.int32, shape, dim)


def nt(a, b, precision=None):
    return lax.dot_general(
        a, b, (((1,), (1,)), ((), ())), preferred_element_type=F32, precision=precision
    )


def tn(a, b, precision=None):
    return lax.dot_general(
        a, b, (((0,), (0,)), ((), ())), preferred_element_type=F32, precision=precision
    )


def nn(a, b, precision=None):
    return jnp.dot(a, b, preferred_element_type=F32, precision=precision)


def bf(mask):
    return mask.astype(F32).astype(BF16)


def kernel(
    owner_ref, local_ref, slot_ref, hop_ref, pos_ref,
    table_hbm, cur_hbm, nw_hbm, cw_hbm, cand_hbm,
    rows_acc, loss_ref, cand_out, ngrad_ref,
    cur_v, curt_v, table_v, nw_v, cw_v, cand_v, mask_v, pgrad_v, x_v, mixed_v, pooled_g,
    ask_send, ask_mid, ask_recv, ids_v, row_out, row_send, row_recv, cols_v,
    emb_send, emb_all, e_v, sc_send, sc_all, eg_send, eg_recv,
    p_send, p_recv, p_own, a1_send, a1_recv, a2_f, a2_send, a2_recv,
    b1_f, b1_send, b1_recv, b2_f, b2_send, b2_recv,
    in_sem, ask_sem, out_ssem, out_rsem, row_ssem, row_rsem,
    emb_sem, sc_sem, eg_sem, p_ssem, p_rsem, a1_ssem, a1_rsem, a2_sem, b1_ssem, b1_rsem, b2_sem,
):
    rep = lax.axis_index("rep")
    neg = lax.axis_index("neg")
    y, core = rep // CORES, lax.rem(rep, CORES)
    x, z = neg // 4, lax.rem(neg, 4)
    mate = (y * CORES + 1 - core, neg)

    def send(src, dst, ssem, rsem, where):
        pltpu.make_async_remote_copy(
            src_ref=src, dst_ref=dst, send_sem=ssem, recv_sem=rsem,
            device_id=where, device_id_type=MESH,
        ).start()

    def settle(ref, sem):
        pltpu.make_async_copy(ref, ref, sem).wait()

    def around(here, count, body):
        def step(i, carry):
            body(lax.rem(here + i, count))
            return carry

        lax.fori_loop(1, count, step, 0)

    loads = [
        pltpu.make_async_copy(cur_hbm, cur_v, in_sem.at[0]),
        pltpu.make_async_copy(table_hbm, table_v, in_sem.at[1]),
        pltpu.make_async_copy(cand_hbm, cand_v.at[pl.ds(0, OWN)], in_sem.at[2]),
        pltpu.make_async_copy(cand_hbm, cand_v.at[pl.ds(OWN, OWN)], in_sem.at[3]),
    ]
    nw_loads = [
        pltpu.make_async_copy(
            nw_hbm.at[:, pl.ds(j * TILE, TILE)], nw_v.at[j], in_sem.at[4 + j]
        )
        for j in range(TILES)
    ]
    cw_loads = [
        pltpu.make_async_copy(
            cw_hbm.at[:, pl.ds(j * TILE, TILE)], cw_v.at[j], in_sem.at[4 + TILES + j]
        )
        for j in range(TILES)
    ]
    loads[0].start()
    for load in nw_loads:
        load.start()
    for load in loads[1:]:
        load.start()
    for load in cw_loads:
        load.start()

    barrier = pltpu.get_barrier_semaphore()

    def greet(where):
        pl.semaphore_signal(barrier, inc=1, device_id=where, device_id_type=MESH)

    around(neg, NEGS, lambda n: greet((rep, n)))
    around(rep, REPS, lambda r: greet((r, neg)))

    owner = owner_ref[...]
    hit = owner == iota((DEVS, REQ), 0)
    hit_low = bf(hit)
    before = bf(iota((REQ, REQ), 0) < iota((REQ, REQ), 1))
    count = nn(hit_low, before)
    rank = jnp.sum(jnp.where(hit, count, 0.0), axis=0, keepdims=True)
    local = local_ref[...].reshape(1, REQ)
    line = iota((DEVS, REQ), 0).astype(F32)
    pay = jnp.where(line == rank, (local >> 5).astype(F32), 0.0) + jnp.where(
        line == rank + 16.0, (local & 31).astype(F32), 0.0
    )
    asks = nt(hit_low, pay.astype(BF16))
    lane1 = iota((1, 128), 1)
    positives = jnp.zeros((1, 128), jnp.int32)
    for t in range(B):
        value = pos_ref[t]
        positives = positives + jnp.where(lane1 == 32 + t, value >> 5, 0)
        positives = positives + jnp.where(lane1 == 36 + t, value & 31, 0)
    asks = asks + positives.astype(F32)
    ask_send[...] = asks.reshape(REPS, NEGS, 1, 128)

    pl.semaphore_wait(barrier, NEGS - 1 + REPS - 1)
    around(
        rep, REPS,
        lambda r: send(
            ask_send.at[r], ask_mid.at[rep], ask_sem.at[0], ask_sem.at[1], (r, neg)
        ),
    )
    ask_mid[rep] = ask_send[rep]

    from_x = (x + 4 - ((owner >> 2) & 3)) & 3
    from_z = (z + 4 - (owner & 3)) & 3
    from_y = (y + 4 - (owner >> 5)) & 3
    turn = (from_x + from_y + from_z) & 3
    placed = turn * 32 + (from_x * 4 + from_z) * 2 + ((owner >> 4) & 1)
    eye = bf(iota((REQ, REQ), 0) == iota((REQ, REQ), 1))
    pair = jnp.where(iota((16, REQ), 0) == 0, placed.astype(F32), rank).astype(BF16)
    cols_v[...] = nt(eye, pair)

    spread = bf(iota((REQ, HOP1), 0) // SLOTS == iota((REQ, HOP1), 1))
    counts = nt(spread, slot_ref[...].astype(F32).astype(BF16))
    at_slot = iota((REQ, SLOTS), 0) % SLOTS == iota((REQ, SLOTS), 1)
    weight = jnp.sum(jnp.where(at_slot, counts, 0.0), axis=1, keepdims=True) / jnp.sum(
        counts, axis=1, keepdims=True
    )

    loads[0].wait()

    def project(j):
        nw_loads[j].wait()
        projected = nn(cur_v[...], nw_v[j])
        mask_v[j] = bf(projected > 0.0)
        weighted = jnp.maximum(projected, 0.0) * weight
        pooled = jnp.sum(weighted.reshape(HOP1, SLOTS, TILE), axis=1)
        x_v[:, F + j * TILE : F + (j + 1) * TILE] = pooled.astype(BF16)

    for j in range(TILES // 2):
        project(j)
    settle(ask_mid.at[pl.ds(0, REPS - 1)], ask_sem.at[1])
    around(
        neg, NEGS,
        lambda n: send(
            ask_mid.at[:, n], ask_recv.at[:, neg], ask_sem.at[2], ask_sem.at[3], (rep, n)
        ),
    )
    ask_recv[:, neg] = ask_mid[:, neg]
    for j in range(TILES // 2, TILES):
        project(j)
    first = bf(iota((HOP1, REQ), 0) * SLOTS == iota((HOP1, REQ), 1))
    x_v[:, 0:F] = nn(first, cur_v[...]).astype(BF16)
    loads[1].wait()
    settle(ask_recv.at[:, pl.ds(0, NEGS - 1)], ask_sem.at[3])
    line_i, line_d = iota((DEVS, DEVS), 0), iota((DEVS, DEVS), 1)
    to_x, to_z = (line_i >> 2) & 3, line_i & 3
    to_y = (y + 8 + (line_i >> 5) - to_x - to_z) & 3
    target = to_y * 32 + ((line_i >> 4) & 1) * 16 + ((x + to_x) & 3) * 4 + ((z + to_z) & 3)
    ids_v[...] = nn(bf(target == line_d), ask_recv[...].reshape(DEVS, 128).astype(BF16))

    def serve(k):
        first_half = pl.multiple_of(k * 32 + (1 - core) * NEGS, NEGS)
        second_half = pl.multiple_of(k * 32 + core * NEGS, NEGS)
        asked = jnp.concatenate(
            [ids_v[pl.ds(first_half, NEGS), :], ids_v[pl.ds(second_half, NEGS), :]], axis=0
        ).astype(BF16)

        def chosen(rows, per, slot_of):
            wide = nn(bf(iota((rows, 32), 0) // per % 32 == iota((rows, 32), 1)), asked)
            slot = slot_of(iota((rows, 1), 0))
            at = iota((rows, 128), 1)
            ids = jnp.sum(
                jnp.where(at == slot, wide * 32.0, 0.0) + jnp.where(at == slot + 16, wide, 0.0),
                axis=1,
                keepdims=True,
            )
            return bf(ids == iota((rows, F), 1).astype(F32))

        main = nn(chosen(512, 16, lambda r: r % 16), table_v[:, 0:WIDE]).reshape(32, 16, WIDE)
        tail = nn(
            chosen(768, 8, lambda r: jnp.maximum(r % 8 - 4, 0) * 3 + r // 256),
            table_v[:, WIDE:F],
        )
        high = iota((32, 8, PART), 1) >= 4
        parts = []
        for c in range(3):
            own = main[:, 8:16, c * PART : (c + 1) * PART]
            parts.append(
                jnp.where(high, tail[256 * c : 256 * (c + 1)].reshape(32, 8, PART), own)
            )
        lower = jnp.concatenate(parts, axis=2)
        block = jnp.concatenate([main[:, 0:8, :], lower], axis=1).astype(BF16)
        row_out[k] = block[0:NEGS]
        send(row_out.at[k], row_send.at[k, :, core], out_ssem.at[k], out_rsem.at[k], mate)
        row_send[k, :, core] = block[NEGS:32]

    def post(k, part):
        def one(i, carry):
            j = lax.rem(i + core * (NEGS - 2 * i), NEGS)
            dx, dz = j // 4, lax.rem(j, 4)
            dy = lax.rem(k + 8 - dx - dz, YS)
            where = (
                lax.rem(y + dy, YS) * CORES + core,
                lax.rem(x + dx, 4) * 4 + lax.rem(z + dz, 4),
            )
            send(row_send.at[k, j], row_recv.at[k, j], row_ssem.at[k], row_rsem.at[k], where)
            return carry

        if part == 0:
            settle(row_out.at[k], out_rsem.at[k])
            if k == 0:
                row_recv[0, 0] = row_send[0, 0]
        lax.fori_loop(8 * part + (1 if k + part == 0 else 0), 8 * part + 8, one, 0)

    serve(0)
    post(0, 0)

    pooled_x = x_v[...]
    for j in range(TILES):
        cw_loads[j].wait()
        mixed_v[:, j * TILE : (j + 1) * TILE] = nn(pooled_x, cw_v[j])
    mixed_in = mixed_v[...]
    mixed = jnp.maximum(mixed_in, 0.0)
    inv_mid = lax.rsqrt(jnp.mean(mixed * mixed, axis=1, keepdims=True) + EPSILON)
    normed = mixed * inv_mid
    top_rows = bf(iota((8, B), 0) == iota((8, B), 1))
    hops = nn(top_rows, hop_ref[...].astype(F32).astype(BF16))
    lanes_of = bf(iota((K1, HOP1), 0) == iota((K1, HOP1), 1) % K1)
    own_hop = iota((8, HOP1), 0) == iota((8, HOP1), 1) // K1
    hop_total = jnp.maximum(jnp.sum(hops, axis=1, keepdims=True), 1.0)
    hop_mat = jnp.where(own_hop, nn(hops.astype(BF16), lanes_of), 0.0) / hop_total
    top_in = nn(hop_mat, normed, HIGH)
    inv_top = lax.rsqrt(jnp.mean(top_in * top_in, axis=1, keepdims=True) + EPSILON)
    embedding = (top_in * inv_top).astype(BF16)
    part = H // 4
    packed = jnp.zeros((16, part), F32)
    for c in range(4):
        move = bf(
            (iota((16, 8), 0) == iota((16, 8), 1) + 4 * c) & (iota((16, 8), 1) < B)
        )
        packed = packed + nn(move, embedding[:, c * part : (c + 1) * part])
    emb_send[...] = packed.astype(BF16)
    around(
        neg, NEGS,
        lambda n: send(emb_send, emb_all.at[neg], emb_sem.at[0], emb_sem.at[1], (rep, n)),
    )
    emb_all[neg] = emb_send[...]

    post(0, 1)
    serve(1)
    loads[2].wait()
    loads[3].wait()
    settle(emb_all.at[pl.ds(0, NEGS - 1)], emb_sem.at[1])

    gathered = emb_all[...].reshape(256, part)
    row_q, col_q = iota((64, 256), 0), iota((64, 256), 1)
    for c in range(4):
        move = bf(col_q == (row_q // 4) * 16 + 4 * c + row_q % 4)
        e_v[:, c * part : (c + 1) * part] = nn(move, gathered).astype(BF16)
    left = iota((32, 128), 1) < OWN
    scores = jnp.where(left, nt(e_v[0:32, :], cand_v[...]), nt(e_v[32:64, :], cand_v[...]))
    sc_send[...] = scores
    around(
        neg, NEGS,
        lambda n: send(sc_send, sc_all.at[neg], sc_sem.at[0], sc_sem.at[1], (rep, n)),
    )
    sc_all[neg] = scores

    post(1, 0)
    serve(2)
    mates = ask_recv[rep].reshape(NEGS, 128).astype(BF16)
    halves = []
    for h in range(2):
        pick = bf(iota((32, NEGS), 0) // B + 8 * h == iota((32, NEGS), 1))
        wide = nn(pick, mates)
        at, t = iota((32, 128), 1), iota((32, 128), 0) % B
        halves.append(
            jnp.sum(
                jnp.where(at == 32 + t, wide * 32.0, 0.0) + jnp.where(at == 36 + t, wide, 0.0),
                axis=1,
                keepdims=True,
            )
        )
    positive = jnp.where(left, halves[0], halves[1])
    settle(sc_all.at[pl.ds(0, NEGS - 1)], sc_sem.at[1])

    def by_half(values):
        first = jnp.sum(jnp.where(left, values, 0.0), axis=1, keepdims=True)
        second = jnp.sum(jnp.where(left, 0.0, values), axis=1, keepdims=True)
        return jnp.where(left, first, second)

    all_scores = sc_all[...]
    shape = (NEGS, 32, 128)
    cand_id = (iota(shape, 0) * OWN + iota(shape, 2) % OWN).astype(F32)
    is_pos = cand_id == positive[None]
    pos_score = by_half(jnp.sum(jnp.where(is_pos, all_scores, 0.0), axis=0))
    gaps = all_scores - pos_score[None] + MARGIN
    small = jnp.exp(-jnp.abs(gaps))
    losses = jnp.maximum(gaps, 0.0) + jnp.log1p(small)
    sigmoid = jnp.where(gaps >= 0.0, 1.0, small) / (1.0 + small)
    loss = by_half(jnp.sum(losses, axis=0)) / (NEGS * OWN)
    totals = by_half(jnp.sum(sigmoid, axis=0))
    own_gap = sc_all[neg] - pos_score + MARGIN
    own_small = jnp.exp(-jnp.abs(own_gap))
    own_sig = jnp.where(own_gap >= 0.0, 1.0, own_small) / (1.0 + own_small)
    own_id = (neg * OWN + iota((32, 128), 1) % OWN).astype(F32)
    score_grad = (own_sig - jnp.where(own_id == positive, totals, 0.0)) / (NEGS * OWN)

    g_left = jnp.where(left, score_grad, 0.0).astype(BF16)
    g_right = jnp.where(left, 0.0, score_grad).astype(BF16)
    eg = jnp.concatenate([nn(g_left, cand_v[...]), nn(g_right, cand_v[...])], axis=0).astype(BF16)
    row_p, col_p = iota((256, 64), 0), iota((256, 64), 1)
    eg_out = jnp.zeros((256, part), F32)
    for c in range(4):
        move = bf((row_p // 16 == col_p // 4) & (row_p % 16 == 4 * c + col_p % 4))
        eg_out = eg_out + nn(move, eg[:, c * part : (c + 1) * part])
    eg_send[...] = eg_out.astype(BF16).reshape(NEGS, 16, part)
    around(
        neg, NEGS,
        lambda n: send(eg_send.at[n], eg_recv.at[neg], eg_sem.at[0], eg_sem.at[1], (rep, n)),
    )
    eg_recv[neg] = eg_send[neg]

    post(1, 1)
    lines = (iota((32, 128), 0) == iota((32, 128), 1) + B * (neg % 8)).astype(F32)
    half = jnp.where(neg // 8 == 0, 0, OWN)
    mine = tn(loss, lines, HIGH)
    loss_ref[...] = jnp.sum(
        jnp.where(iota((128, 128), 0) == half, mine, 0.0), axis=0, keepdims=True
    )[:, 0:B]
    cand_out[...] = tn(g_left, e_v[0:32, :])[0:OWN] + tn(g_right, e_v[32:64, :])[OWN:128]
    for b in range(8):
        curt_v[b % 2, 128 * (b // 2) : 128 * (b // 2) + 128, :] = (
            cur_v[:, 128 * b : 128 * b + 128].astype(F32).T.astype(BF16)
        )
    settle(eg_recv.at[pl.ds(0, NEGS - 1)], eg_sem.at[1])
    eg_sum = jnp.sum(eg_recv[...].astype(F32), axis=0)
    embed_grad = []
    for c in range(4):
        move = (
            (iota((8, 16), 1) == iota((8, 16), 0) + 4 * c) & (iota((8, 16), 0) < B)
        ).astype(F32)
        embed_grad.append(nn(move, eg_sum, HIGH))
    embed_grad = jnp.concatenate(embed_grad, axis=1)

    post(2, 0)

    top_grad = inv_top * embed_grad - top_in * (
        inv_top * inv_top * inv_top * jnp.mean(embed_grad * top_in, axis=1, keepdims=True)
    )
    normed_grad = tn(hop_mat, top_grad, HIGH)
    mixed_grad = inv_mid * normed_grad - mixed * (
        inv_mid * inv_mid * inv_mid * jnp.mean(normed_grad * mixed, axis=1, keepdims=True)
    )
    mixed_in_grad = jnp.where(mixed_in > 0.0, mixed_grad, 0.0).astype(BF16)
    total = jnp.zeros((HOP1, H), F32)
    for j in range(TILES):
        total = total + nt(mixed_in_grad[:, j * TILE : (j + 1) * TILE], cw_v[j, F : F + H, :])
    pooled_g[...] = total

    order = (0, 2, 1, 3)
    for j in order:
        spread_grad = jnp.broadcast_to(
            pooled_g[:, j * TILE : (j + 1) * TILE][:, None, :], (HOP1, SLOTS, TILE)
        ).reshape(REQ, TILE)
        pgrad_v[...] = jnp.where(mask_v[j].astype(F32) > 0.0, spread_grad * weight, 0.0).astype(
            BF16
        )
        p_send[j] = nn(curt_v[1 - core], pgrad_v[...]).astype(BF16)
        send(p_send.at[j], p_recv.at[j], p_ssem.at[j], p_rsem.at[j], mate)
        p_own[j] = nn(curt_v[core], pgrad_v[...])

    post(2, 1)

    for j in order:
        settle(p_recv.at[j], p_rsem.at[j])
        chip_sum = p_own[j] + p_recv[j].astype(F32)
        if j < 2:
            a1_send[j] = chip_sum.astype(BF16).reshape(YS, 128, TILE)
            around(
                y, YS,
                lambda q, j=j: send(
                    a1_send.at[j, q], a1_recv.at[j, y], a1_ssem.at[j], a1_rsem.at[j],
                    (q * CORES + core, neg),
                ),
            )
            a1_recv[j, y] = a1_send[j, y]
        else:
            k = j - 2
            for q in range(YS):
                b1_f[:, 8 * q : 8 * q + 8, :] = chip_sum[128 * q : 128 * q + 128].reshape(
                    NEGS, 8, TILE
                )
            b1_send[k] = b1_f[...].astype(BF16)
            around(
                neg, NEGS,
                lambda n, k=k: send(
                    b1_send.at[k, n], b1_recv.at[k, neg], b1_ssem.at[k], b1_rsem.at[k], (rep, n)
                ),
            )
            b1_recv[k, neg] = b1_send[k, neg]

    owner_col = cols_v[:, 0:1]
    rank_col = cols_v[:, 1:2]
    third = jnp.floor((rank_col + 0.5) * (1.0 / 3.0))
    left_over = rank_col - 3.0 * third
    slot_main = owner_col * 16.0 + rank_col
    slot_tail = [
        jnp.where(left_over == float(c), owner_col * 16.0 + 12.0 + third, -1.0) for c in range(3)
    ]

    def place(k):
        settle(row_recv.at[k, pl.ds(0, NEGS - 1 if k == 0 else NEGS)], row_rsem.at[k])
        block = row_recv[k].reshape(512, WIDE)
        line = (iota((REQ, 512), 1) + k * 512).astype(F32)
        body = nn(bf(line == slot_main), block)
        tail = jnp.zeros((REQ, PART), F32)
        for c in range(3):
            tail = tail + nn(bf(line == slot_tail[c]), block[:, c * PART : (c + 1) * PART])
        new = jnp.concatenate([body, tail], axis=1).astype(BF16)
        rows_acc[...] = new if k == 0 else rows_acc[...] + new

    serve(3)
    post(3, 0)
    place(0)
    place(1)

    for j in range(2):
        settle(a1_recv.at[j, pl.ds(0, YS - 1)], a1_rsem.at[j])
        a2_f[:, 8 * j : 8 * j + 8, :] = jnp.sum(a1_recv[j].astype(F32), axis=0).reshape(
            NEGS, 8, TILE
        )
    a2_send[...] = a2_f[...].astype(BF16)
    around(
        neg, NEGS,
        lambda n: send(a2_send.at[n], a2_recv.at[neg], a2_sem.at[0], a2_sem.at[1], (rep, n)),
    )
    a2_recv[neg] = a2_send[neg]
    for k in range(2):
        settle(b1_recv.at[k, pl.ds(0, NEGS - 1)], b1_rsem.at[k])
        b2_f[:, 8 * k : 8 * k + 8, :] = jnp.sum(b1_recv[k].astype(F32), axis=0).reshape(
            YS, 8, TILE
        )
    b2_send[...] = b2_f[...].astype(BF16)
    around(
        y, YS,
        lambda q: send(
            b2_send.at[q], b2_recv.at[y], b2_sem.at[0], b2_sem.at[1], (q * CORES + core, neg)
        ),
    )
    b2_recv[y] = b2_send[y]

    post(3, 1)
    place(2)
    place(3)
    settle(a2_recv.at[pl.ds(0, NEGS - 1)], a2_sem.at[1])
    a_sum = jnp.sum(a2_recv[...].astype(F32), axis=0)
    settle(b2_recv.at[pl.ds(0, YS - 1)], b2_sem.at[1])
    b_sum = jnp.sum(b2_recv[...].astype(F32), axis=0)
    for j in range(2):
        ngrad_ref[:, j * TILE : (j + 1) * TILE] = a_sum[8 * j : 8 * j + 8]
        ngrad_ref[:, (j + 2) * TILE : (j + 3) * TILE] = b_sum[8 * j : 8 * j + 8]

    settle(ask_send.at[pl.ds(0, REPS - 1)], ask_sem.at[0])
    settle(ask_mid.at[:, pl.ds(0, NEGS - 1)], ask_sem.at[2])
    for k in range(YS):
        settle(row_out.at[k], out_ssem.at[k])
        settle(row_send.at[k, pl.ds(0, NEGS - 1 if k == 0 else NEGS)], row_ssem.at[k])
    settle(emb_all.at[pl.ds(0, NEGS - 1)], emb_sem.at[0])
    settle(sc_all.at[pl.ds(0, NEGS - 1)], sc_sem.at[0])
    settle(eg_send.at[pl.ds(0, NEGS - 1)], eg_sem.at[0])
    for j in range(TILES):
        settle(p_send.at[j], p_ssem.at[j])
    for j in range(2):
        settle(a1_send.at[j, pl.ds(0, YS - 1)], a1_ssem.at[j])
        settle(b1_send.at[j, pl.ds(0, NEGS - 1)], b1_ssem.at[j])
    settle(a2_send.at[pl.ds(0, NEGS - 1)], a2_sem.at[0])
    settle(b2_send.at[pl.ds(0, YS - 1)], b2_sem.at[0])


def local(
    feature_table, cur_rows, next_owner, next_local, slot_counts, hop_counts, positive_ids,
    neighbor_weight, combine_weight, candidates,
):
    vmem = pl.BlockSpec(memory_space=pltpu.VMEM)
    smem = pl.BlockSpec(memory_space=pltpu.SMEM)
    hbm = pl.BlockSpec(memory_space=pl.ANY)
    dma = pltpu.SemaphoreType.DMA
    part = H // 4
    scratch = [
        pltpu.VMEM((REQ, F), BF16),
        pltpu.VMEM((2, 512, REQ), BF16),
        pltpu.VMEM((F, F), BF16),
        pltpu.VMEM((TILES, F, TILE), BF16),
        pltpu.VMEM((TILES, F + H, TILE), BF16),
        pltpu.VMEM((2 * OWN, H), BF16),
        pltpu.VMEM((TILES, REQ, TILE), BF16),
        pltpu.VMEM((REQ, TILE), BF16),
        pltpu.VMEM((HOP1, F + H), BF16),
        pltpu.VMEM((HOP1, H), F32),
        pltpu.VMEM((HOP1, H), F32),
        pltpu.VMEM((REPS, NEGS, 1, 128), F32),
        pltpu.VMEM((REPS, NEGS, 1, 128), F32),
        pltpu.VMEM((REPS, NEGS, 1, 128), F32),
        pltpu.VMEM((DEVS, 128), F32),
        pltpu.VMEM((YS, NEGS, 16, WIDE), BF16),
        pltpu.VMEM((YS, NEGS, CORES, 16, WIDE), BF16),
        pltpu.VMEM((YS, NEGS, CORES, 16, WIDE), BF16),
        pltpu.VMEM((REQ, 16), F32),
        pltpu.VMEM((16, part), BF16),
        pltpu.VMEM((NEGS, 16, part), BF16),
        pltpu.VMEM((64, H), BF16),
        pltpu.VMEM((32, 128), F32),
        pltpu.VMEM((NEGS, 32, 128), F32),
        pltpu.VMEM((NEGS, 16, part), BF16),
        pltpu.VMEM((NEGS, 16, part), BF16),
        pltpu.VMEM((TILES, 512, TILE), BF16),
        pltpu.VMEM((TILES, 512, TILE), BF16),
        pltpu.VMEM((TILES, 512, TILE), F32),
        pltpu.VMEM((2, YS, 128, TILE), BF16),
        pltpu.VMEM((2, YS, 128, TILE), BF16),
        pltpu.VMEM((NEGS, 16, TILE), F32),
        pltpu.VMEM((NEGS, 16, TILE), BF16),
        pltpu.VMEM((NEGS, 16, TILE), BF16),
        pltpu.VMEM((NEGS, 32, TILE), F32),
        pltpu.VMEM((2, NEGS, 32, TILE), BF16),
        pltpu.VMEM((2, NEGS, 32, TILE), BF16),
        pltpu.VMEM((YS, 16, TILE), F32),
        pltpu.VMEM((YS, 16, TILE), BF16),
        pltpu.VMEM((YS, 16, TILE), BF16),
        dma((4 + 2 * TILES,)),
        dma((4,)), dma((YS,)), dma((YS,)), dma((YS,)), dma((YS,)),
        dma((2,)), dma((2,)), dma((2,)),
        dma((TILES,)), dma((TILES,)),
        dma((2,)), dma((2,)), dma((2,)),
        dma((2,)), dma((2,)), dma((2,)),
    ]
    next_rows, loss, cand_grad, neighbor_grad = pl.pallas_call(
        kernel,
        out_shape=(
            pltpu.VMEM((REQ, F), BF16),
            pltpu.VMEM((1, B), F32),
            pltpu.VMEM((OWN, H), F32),
            pltpu.VMEM((8, H), F32),
        ),
        in_specs=[vmem, vmem, vmem, vmem, smem, hbm, hbm, hbm, hbm, hbm],
        out_specs=(vmem, vmem, vmem, vmem),
        scratch_shapes=scratch,
        compiler_params=pltpu.CompilerParams(
            collective_id=0, has_side_effects=True, vmem_limit_bytes=58 * 2**20
        ),
        name="step",
    )(
        next_owner.reshape(1, REQ),
        next_local,
        slot_counts.T,
        hop_counts,
        positive_ids,
        feature_table,
        cur_rows,
        neighbor_weight,
        combine_weight,
        candidates,
    )
    return next_rows, loss.reshape(B), cand_grad, neighbor_grad


def solution(mesh):
    both = P(("rep", "neg"), None)
    flat = P(("rep", "neg"))
    return jax.shard_map(
        local,
        mesh=mesh,
        in_specs=(both, both, both, flat, both, both, flat, P(), P(), both),
        out_specs=(both, flat, both, both),
        check_vma=False,
    )
```

```python
import jax
import jax.numpy as jnp
from jax import lax
from jax.experimental import pallas as pl
from jax.experimental.pallas import tpu as pltpu
from jax.sharding import PartitionSpec as P

EPSILON = 1e-06
MARGIN = 0.5
MESH = pl.DeviceIdType.MESH
F32 = jnp.float32
BF16 = jnp.bfloat16
HIGH = lax.Precision.HIGHEST

REPS, NEGS, DEVS = 8, 16, 128
YS, CORES = 4, 2
F, H = 1024, 2048
TILE = 512
TILES = H // TILE
REQ, HOP1, SLOTS, B, K1 = 768, 48, 16, 4, 12
PART = 256
WIDE = 3 * PART
OWN = 64
COLS = ((0, 768), (768, 1408), (1408, 2048))
ORDERS = ((0, 1, 2), (1, 2, 0), (2, 0, 1))
STOPS = (16, 28, 40, 52, 60, 64, 64, 64)


def iota(shape, dim):
    return lax.broadcasted_iota(jnp.int32, shape, dim)


def nt(a, b, precision=None):
    return lax.dot_general(
        a, b, (((1,), (1,)), ((), ())), preferred_element_type=F32, precision=precision
    )


def tn(a, b, precision=None):
    return lax.dot_general(
        a, b, (((0,), (0,)), ((), ())), preferred_element_type=F32, precision=precision
    )


def nn(a, b, precision=None):
    return jnp.dot(a, b, preferred_element_type=F32, precision=precision)


def bf(mask):
    return mask.astype(F32).astype(BF16)


def kernel(
    owner_ref, local_ref, slot_ref, hop_ref, pos_ref,
    table_hbm, cur_hbm, nw_hbm, cw_hbm, cand_hbm,
    rows_acc, loss_ref, cand_out, ngrad_ref,
    cur_v, curt_v, table_v, nw_v, cw_v, cand_v, mask_v, pgrad_v, x_v, mixed_v, pooled_g,
    ask_send, ask_mid, ask_recv, ids_v, row_out, row_send, row_recv, cols_v,
    emb_send, emb_all, e_v, sc_send, sc_all, eg_send, eg_recv,
    p_send, p_recv, p_own, s1_send, s1_recv, s2_send, s2_recv, s3_send, s3_recv,
    in_sem, ask_sem, out_ssem, out_rsem, row_ssem, row_rsem,
    emb_sem, sc_sem, eg_sem, p_ssem, p_rsem, s_ssem, s_rsem,
):
    rep = lax.axis_index("rep")
    neg = lax.axis_index("neg")
    y, core = rep // CORES, lax.rem(rep, CORES)
    x, z = neg // 4, lax.rem(neg, 4)
    mate = (y * CORES + 1 - core, neg)

    def send(src, dst, ssem, rsem, where):
        pltpu.make_async_remote_copy(
            src_ref=src, dst_ref=dst, send_sem=ssem, recv_sem=rsem,
            device_id=where, device_id_type=MESH,
        ).start()

    def settle(ref, sem):
        pltpu.make_async_copy(ref, ref, sem).wait()

    def around(here, count, body):
        def step(i, carry):
            body(lax.rem(here + i, count))
            return carry

        lax.fori_loop(1, count, step, 0)

    barrier = pltpu.get_barrier_semaphore()

    def greet(where):
        pl.semaphore_signal(barrier, inc=1, device_id=where, device_id_type=MESH)

    around(neg, NEGS, lambda n: greet((rep, n)))
    around(rep, REPS, lambda r: greet((r, neg)))

    loads = [
        pltpu.make_async_copy(cur_hbm, cur_v, in_sem.at[0]),
        pltpu.make_async_copy(table_hbm, table_v, in_sem.at[1]),
        pltpu.make_async_copy(cand_hbm, cand_v.at[pl.ds(0, OWN)], in_sem.at[2]),
        pltpu.make_async_copy(cand_hbm, cand_v.at[pl.ds(OWN, OWN)], in_sem.at[3]),
    ]
    nw_loads = [
        pltpu.make_async_copy(
            nw_hbm.at[:, pl.ds(j * TILE, TILE)], nw_v.at[j], in_sem.at[4 + j]
        )
        for j in range(TILES)
    ]
    cw_loads = [
        pltpu.make_async_copy(
            cw_hbm.at[:, pl.ds(j * TILE, TILE)], cw_v.at[j], in_sem.at[4 + TILES + j]
        )
        for j in range(TILES)
    ]
    loads[0].start()
    for load in nw_loads:
        load.start()
    for load in loads[1:]:
        load.start()
    for load in cw_loads:
        load.start()

    owner = owner_ref[...]
    hit = owner == iota((DEVS, REQ), 0)
    hit_low = bf(hit)
    before = bf(iota((REQ, REQ), 0) < iota((REQ, REQ), 1))
    count = nn(hit_low, before)
    rank = jnp.sum(jnp.where(hit, count, 0.0), axis=0, keepdims=True)
    local = local_ref[...].reshape(1, REQ)
    line = iota((DEVS, REQ), 0).astype(F32)
    pay = jnp.where(line == rank, (local >> 5).astype(F32), 0.0) + jnp.where(
        line == rank + 16.0, (local & 31).astype(F32), 0.0
    )
    asks = nt(hit_low, pay.astype(BF16))
    lane1 = iota((1, 128), 1)
    positives = jnp.zeros((1, 128), jnp.int32)
    for t in range(B):
        value = pos_ref[t]
        positives = positives + jnp.where(lane1 == 32 + t, value >> 5, 0)
        positives = positives + jnp.where(lane1 == 36 + t, value & 31, 0)
    asks = asks + positives.astype(F32)
    ask_send[...] = asks.reshape(REPS, NEGS, 1, 128)

    pl.semaphore_wait(barrier, NEGS - 1 + REPS - 1)
    around(
        rep, REPS,
        lambda r: send(
            ask_send.at[r], ask_mid.at[rep], ask_sem.at[0], ask_sem.at[1], (r, neg)
        ),
    )
    ask_mid[rep] = ask_send[rep]

    from_x = (x + 4 - ((owner >> 2) & 3)) & 3
    from_z = (z + 4 - (owner & 3)) & 3
    from_y = (y + 4 - (owner >> 5)) & 3
    turn = (from_x + from_y + from_z) & 3
    placed = turn * 32 + (from_x * 4 + from_z) * 2 + ((owner >> 4) & 1)
    eye = bf(iota((REQ, REQ), 0) == iota((REQ, REQ), 1))
    pair = jnp.where(iota((16, REQ), 0) == 0, placed.astype(F32), rank).astype(BF16)
    cols_v[...] = nt(eye, pair)

    spread = bf(iota((REQ, HOP1), 0) // SLOTS == iota((REQ, HOP1), 1))
    counts = nt(spread, slot_ref[...].astype(F32).astype(BF16))
    at_slot = iota((REQ, SLOTS), 0) % SLOTS == iota((REQ, SLOTS), 1)
    weight = jnp.sum(jnp.where(at_slot, counts, 0.0), axis=1, keepdims=True) / jnp.sum(
        counts, axis=1, keepdims=True
    )

    loads[0].wait()

    def project(j):
        nw_loads[j].wait()
        projected = nn(cur_v[...], nw_v[j])
        mask_v[:, j * TILE : (j + 1) * TILE] = bf(projected > 0.0)
        weighted = jnp.maximum(projected, 0.0) * weight
        pooled = jnp.sum(weighted.reshape(HOP1, SLOTS, TILE), axis=1)
        x_v[:, F + j * TILE : F + (j + 1) * TILE] = pooled.astype(BF16)

    settle(ask_mid.at[pl.ds(0, REPS - 1)], ask_sem.at[1])
    around(
        neg, NEGS,
        lambda n: send(
            ask_mid.at[:, n], ask_recv.at[:, neg], ask_sem.at[2], ask_sem.at[3], (rep, n)
        ),
    )
    ask_recv[:, neg] = ask_mid[:, neg]
    for j in range(TILES // 2):
        project(j)
    loads[1].wait()
    settle(ask_recv.at[:, pl.ds(0, NEGS - 1)], ask_sem.at[3])
    line_i, line_d = iota((DEVS, DEVS), 0), iota((DEVS, DEVS), 1)
    to_x, to_z = (line_i >> 2) & 3, line_i & 3
    to_y = (y + 8 + (line_i >> 5) - to_x - to_z) & 3
    target = to_y * 32 + ((line_i >> 4) & 1) * 16 + ((x + to_x) & 3) * 4 + ((z + to_z) & 3)
    ids_v[...] = nn(bf(target == line_d), ask_recv[...].reshape(DEVS, 128).astype(BF16))

    def serve(k):
        first_half = pl.multiple_of(k * 32 + (1 - core) * NEGS, NEGS)
        second_half = pl.multiple_of(k * 32 + core * NEGS, NEGS)
        asked = jnp.concatenate(
            [ids_v[pl.ds(first_half, NEGS), :], ids_v[pl.ds(second_half, NEGS), :]], axis=0
        ).astype(BF16)

        def chosen(rows, per, slot_of):
            wide = nn(bf(iota((rows, 32), 0) // per % 32 == iota((rows, 32), 1)), asked)
            slot = slot_of(iota((rows, 1), 0))
            at = iota((rows, 128), 1)
            ids = jnp.sum(
                jnp.where(at == slot, wide * 32.0, 0.0) + jnp.where(at == slot + 16, wide, 0.0),
                axis=1,
                keepdims=True,
            )
            return bf(ids == iota((rows, F), 1).astype(F32))

        main = nn(chosen(512, 16, lambda r: r % 16), table_v[:, 0:WIDE]).reshape(32, 16, WIDE)
        tail = nn(
            chosen(768, 8, lambda r: jnp.maximum(r % 8 - 4, 0) * 3 + r // 256),
            table_v[:, WIDE:F],
        )
        high = iota((32, 8, PART), 1) >= 4
        parts = []
        for c in range(3):
            own = main[:, 8:16, c * PART : (c + 1) * PART]
            parts.append(
                jnp.where(high, tail[256 * c : 256 * (c + 1)].reshape(32, 8, PART), own)
            )
        lower = jnp.concatenate(parts, axis=2)
        block = jnp.concatenate([main[:, 0:8, :], lower], axis=1).astype(BF16)
        row_out[k] = block[0:NEGS]
        send(row_out.at[k], row_send.at[k, :, core], out_ssem.at[k], out_rsem.at[k], mate)
        row_send[k, :, core] = block[NEGS:32]

    done = {"sent": 0, "served": 0}

    def serve_to(rounds):
        while done["served"] < rounds:
            serve(done["served"])
            done["served"] += 1

    def post_to(limit, rounds=0):
        while done["sent"] < limit:
            k = done["sent"] // NEGS
            serve_to(k + 1)
            low, high = done["sent"] - k * NEGS, min(limit - k * NEGS, NEGS)
            done["sent"] = k * NEGS + high

            def one(i, carry):
                j = lax.rem(i + core * (NEGS - 2 * i), NEGS)
                dx, dz = j // 4, lax.rem(j, 4)
                dy = lax.rem(k + 8 - dx - dz, YS)
                where = (
                    lax.rem(y + dy, YS) * CORES + core,
                    lax.rem(x + dx, 4) * 4 + lax.rem(z + dz, 4),
                )
                send(
                    row_send.at[k, j], row_recv.at[k, j], row_ssem.at[k], row_rsem.at[k], where
                )
                return carry

            if low == 0:
                settle(row_out.at[k], out_rsem.at[k])
                if k == 0:
                    row_recv[0, 0] = row_send[0, 0]
                    low = 1
            lax.fori_loop(low, high, one, 0)
        serve_to(rounds)

    post_to(STOPS[0], 1)
    for j in range(TILES // 2, TILES):
        project(j)
    first = bf(iota((HOP1, REQ), 0) * SLOTS == iota((HOP1, REQ), 1))
    x_v[:, 0:F] = nn(first, cur_v[...]).astype(BF16)

    pooled_x = x_v[...]
    for j in range(TILES):
        cw_loads[j].wait()
        mixed_v[:, j * TILE : (j + 1) * TILE] = nn(pooled_x, cw_v[j])
    mixed_in = mixed_v[...]
    mixed = jnp.maximum(mixed_in, 0.0)
    inv_mid = lax.rsqrt(jnp.mean(mixed * mixed, axis=1, keepdims=True) + EPSILON)
    normed = mixed * inv_mid
    top_rows = bf(iota((8, B), 0) == iota((8, B), 1))
    hops = nn(top_rows, hop_ref[...].astype(F32).astype(BF16))
    lanes_of = bf(iota((K1, HOP1), 0) == iota((K1, HOP1), 1) % K1)
    own_hop = iota((8, HOP1), 0) == iota((8, HOP1), 1) // K1
    hop_total = jnp.maximum(jnp.sum(hops, axis=1, keepdims=True), 1.0)
    hop_mat = jnp.where(own_hop, nn(hops.astype(BF16), lanes_of), 0.0) / hop_total
    top_in = nn(hop_mat, normed, HIGH)
    inv_top = lax.rsqrt(jnp.mean(top_in * top_in, axis=1, keepdims=True) + EPSILON)
    embedding = (top_in * inv_top).astype(BF16)
    part = H // 4
    packed = jnp.zeros((16, part), F32)
    for c in range(4):
        move = bf(
            (iota((16, 8), 0) == iota((16, 8), 1) + 4 * c) & (iota((16, 8), 1) < B)
        )
        packed = packed + nn(move, embedding[:, c * part : (c + 1) * part])
    emb_send[...] = packed.astype(BF16)
    around(
        neg, NEGS,
        lambda n: send(emb_send, emb_all.at[neg], emb_sem.at[0], emb_sem.at[1], (rep, n)),
    )
    emb_all[neg] = emb_send[...]

    post_to(STOPS[1], 2)
    loads[2].wait()
    loads[3].wait()
    settle(emb_all.at[pl.ds(0, NEGS - 1)], emb_sem.at[1])

    gathered = emb_all[...].reshape(256, part)
    row_q, col_q = iota((64, 256), 0), iota((64, 256), 1)
    for c in range(4):
        move = bf(col_q == (row_q // 4) * 16 + 4 * c + row_q % 4)
        e_v[:, c * part : (c + 1) * part] = nn(move, gathered).astype(BF16)
    left = iota((32, 128), 1) < OWN
    scores = jnp.where(left, nt(e_v[0:32, :], cand_v[...]), nt(e_v[32:64, :], cand_v[...]))
    sc_send[...] = scores
    around(
        neg, NEGS,
        lambda n: send(sc_send, sc_all.at[neg], sc_sem.at[0], sc_sem.at[1], (rep, n)),
    )
    sc_all[neg] = scores

    post_to(STOPS[2], 3)
    mates = ask_recv[rep].reshape(NEGS, 128).astype(BF16)
    halves = []
    for h in range(2):
        pick = bf(iota((32, NEGS), 0) // B + 8 * h == iota((32, NEGS), 1))
        wide = nn(pick, mates)
        at, t = iota((32, 128), 1), iota((32, 128), 0) % B
        halves.append(
            jnp.sum(
                jnp.where(at == 32 + t, wide * 32.0, 0.0) + jnp.where(at == 36 + t, wide, 0.0),
                axis=1,
                keepdims=True,
            )
        )
    positive = jnp.where(left, halves[0], halves[1])
    settle(sc_all.at[pl.ds(0, NEGS - 1)], sc_sem.at[1])

    def by_half(values):
        first = jnp.sum(jnp.where(left, values, 0.0), axis=1, keepdims=True)
        second = jnp.sum(jnp.where(left, 0.0, values), axis=1, keepdims=True)
        return jnp.where(left, first, second)

    all_scores = sc_all[...]
    shape = (NEGS, 32, 128)
    cand_id = (iota(shape, 0) * OWN + iota(shape, 2) % OWN).astype(F32)
    is_pos = cand_id == positive[None]
    pos_score = by_half(jnp.sum(jnp.where(is_pos, all_scores, 0.0), axis=0))
    gaps = all_scores - pos_score[None] + MARGIN
    small = jnp.exp(-jnp.abs(gaps))
    losses = jnp.maximum(gaps, 0.0) + jnp.log1p(small)
    sigmoid = jnp.where(gaps >= 0.0, 1.0, small) / (1.0 + small)
    loss = by_half(jnp.sum(losses, axis=0)) / (NEGS * OWN)
    totals = by_half(jnp.sum(sigmoid, axis=0))
    own_gap = sc_all[neg] - pos_score + MARGIN
    own_small = jnp.exp(-jnp.abs(own_gap))
    own_sig = jnp.where(own_gap >= 0.0, 1.0, own_small) / (1.0 + own_small)
    own_id = (neg * OWN + iota((32, 128), 1) % OWN).astype(F32)
    score_grad = (own_sig - jnp.where(own_id == positive, totals, 0.0)) / (NEGS * OWN)

    g_left = jnp.where(left, score_grad, 0.0).astype(BF16)
    g_right = jnp.where(left, 0.0, score_grad).astype(BF16)
    eg = jnp.concatenate([nn(g_left, cand_v[...]), nn(g_right, cand_v[...])], axis=0).astype(BF16)
    row_p, col_p = iota((256, 64), 0), iota((256, 64), 1)
    eg_out = jnp.zeros((256, part), F32)
    for c in range(4):
        move = bf((row_p // 16 == col_p // 4) & (row_p % 16 == 4 * c + col_p % 4))
        eg_out = eg_out + nn(move, eg[:, c * part : (c + 1) * part])
    eg_send[...] = eg_out.astype(BF16).reshape(NEGS, 16, part)
    around(
        neg, NEGS,
        lambda n: send(eg_send.at[n], eg_recv.at[neg], eg_sem.at[0], eg_sem.at[1], (rep, n)),
    )
    eg_recv[neg] = eg_send[neg]

    post_to(STOPS[3], 4)
    for b in range(8):
        curt_v[0, b % 2, 128 * (b // 2) : 128 * (b // 2) + 128, :] = (
            cur_v[:, 128 * b : 128 * b + 128].astype(F32).T.astype(BF16)
        )
    r, source = iota((512, 512), 0), iota((512, 512), 1)
    high, middle, low = r >> 7, (r >> 5) & 3, (r >> 3) & 3
    for t, rows_from in (
        (1, low * 128 + high * 32 + middle * 8 + (r & 7)),
        (2, middle * 128 + low * 32 + high * 8 + (r & 7)),
    ):
        move = bf(rows_from == source)
        for c in range(CORES):
            curt_v[t, c] = nn(move, curt_v[0, c]).astype(BF16)
    settle(eg_recv.at[pl.ds(0, NEGS - 1)], eg_sem.at[1])
    eg_sum = jnp.sum(eg_recv[...].astype(F32), axis=0)
    embed_grad = []
    for c in range(4):
        move = (
            (iota((8, 16), 1) == iota((8, 16), 0) + 4 * c) & (iota((8, 16), 0) < B)
        ).astype(F32)
        embed_grad.append(nn(move, eg_sum, HIGH))
    embed_grad = jnp.concatenate(embed_grad, axis=1)

    post_to(STOPS[4])

    top_grad = inv_top * embed_grad - top_in * (
        inv_top * inv_top * inv_top * jnp.mean(embed_grad * top_in, axis=1, keepdims=True)
    )
    normed_grad = tn(hop_mat, top_grad, HIGH)
    mixed_grad = inv_mid * normed_grad - mixed * (
        inv_mid * inv_mid * inv_mid * jnp.mean(normed_grad * mixed, axis=1, keepdims=True)
    )
    mixed_in_grad = jnp.where(mixed_in > 0.0, mixed_grad, 0.0).astype(BF16)
    total = jnp.zeros((HOP1, H), F32)
    for j in range(TILES):
        total = total + nt(mixed_in_grad[:, j * TILE : (j + 1) * TILE], cw_v[j, F : F + H, :])
    pooled_g[...] = total

    post_to(STOPS[5])

    def products(t, slot):
        low, high = COLS[t]
        width = high - low
        spread_grad = jnp.broadcast_to(
            pooled_g[:, low:high][:, None, :], (HOP1, SLOTS, width)
        ).reshape(REQ, width)
        pgrad_v[slot, :, 0:width] = jnp.where(
            mask_v[:, low:high].astype(F32) > 0.0, spread_grad * weight, 0.0
        ).astype(BF16)
        p_send[:, low:high] = nn(curt_v[t, 1 - core], pgrad_v[slot, :, 0:width]).astype(BF16)
        cols = pl.ds(low, width)
        send(p_send.at[:, cols], p_recv.at[:, cols], p_ssem.at[t], p_rsem.at[t], mate)
        p_own[slot, :, 0:width] = nn(curt_v[t, core], pgrad_v[slot, :, 0:width])

    here = (y, x, z)

    def along(axis, body):
        def one(q):
            where = ((q * CORES + core, neg), (rep, q * 4 + z), (rep, x * 4 + q))[axis]
            body(q, where)

        around(here[axis], YS, one)

    stages = ((s1_send, s1_recv), (s2_send, s2_recv), (s3_send, s3_recv))

    def scatter(t, stage, total):
        low, high = COLS[t]
        width, axis = high - low, ORDERS[t][stage]
        out, back = stages[stage]
        cols = pl.ds(0, width)
        rows = out.shape[2]
        out[t, :, :, 0:width] = total.astype(out.dtype).reshape(YS, rows, width)
        along(
            axis,
            lambda q, where: send(
                out.at[t, q, :, cols], back.at[t, here[axis], :, cols],
                s_ssem.at[stage, t], s_rsem.at[stage, t], where,
            ),
        )
        back[t, here[axis], :, 0:width] = out[t, here[axis], :, 0:width]

    def gather(t, stage):
        low, high = COLS[t]
        width = high - low
        back = stages[stage][1]
        settle(back.at[t, pl.ds(0, YS - 1), :, pl.ds(0, width)], s_rsem.at[stage, t])
        return jnp.sum(back[t, :, :, 0:width].astype(F32), axis=0)

    def pass_on(t, slot):
        low, high = COLS[t]
        settle(p_recv.at[:, pl.ds(low, high - low)], p_rsem.at[t])
        scatter(t, 0, p_own[slot, :, 0 : high - low] + p_recv[:, low:high].astype(F32))

    for t in range(3):
        products(t, t % 2)
        if t > 0:
            pass_on(t - 1, (t - 1) % 2)
    pass_on(2, 0)
    post_to(STOPS[6])

    owner_col = cols_v[:, 0:1]
    rank_col = cols_v[:, 1:2]
    third = jnp.floor((rank_col + 0.5) * (1.0 / 3.0))
    left_over = rank_col - 3.0 * third
    slot_main = owner_col * 16.0 + rank_col
    slot_tail = [
        jnp.where(left_over == float(c), owner_col * 16.0 + 12.0 + third, -1.0) for c in range(3)
    ]

    def place(k):
        settle(row_recv.at[k, pl.ds(0, NEGS - 1 if k == 0 else NEGS)], row_rsem.at[k])
        block = row_recv[k].reshape(512, WIDE)
        line = (iota((REQ, 512), 1) + k * 512).astype(F32)
        body = nn(bf(line == slot_main), block)
        tail = jnp.zeros((REQ, PART), F32)
        for c in range(3):
            tail = tail + nn(bf(line == slot_tail[c]), block[:, c * PART : (c + 1) * PART])
        new = jnp.concatenate([body, tail], axis=1).astype(BF16)
        rows_acc[...] = new if k == 0 else rows_acc[...] + new

    lines = (iota((32, 128), 0) == iota((32, 128), 1) + B * (neg % 8)).astype(F32)
    half = jnp.where(neg // 8 == 0, 0, OWN)
    mine = tn(loss, lines, HIGH)
    loss_ref[...] = jnp.sum(
        jnp.where(iota((128, 128), 0) == half, mine, 0.0), axis=0, keepdims=True
    )[:, 0:B]
    cand_out[...] = tn(g_left, e_v[0:32, :])[0:OWN] + tn(g_right, e_v[32:64, :])[OWN:128]
    place(0)

    for t in range(3):
        scatter(t, 1, gather(t, 0))
    post_to(STOPS[7])
    place(1)
    for t in range(3):
        scatter(t, 2, gather(t, 1))
    place(2)
    for t in range(3):
        ngrad_ref[:, COLS[t][0] : COLS[t][1]] = gather(t, 2)
    place(3)

    settle(ask_send.at[pl.ds(0, REPS - 1)], ask_sem.at[0])
    settle(ask_mid.at[:, pl.ds(0, NEGS - 1)], ask_sem.at[2])
    for k in range(YS):
        settle(row_out.at[k], out_ssem.at[k])
        settle(row_send.at[k, pl.ds(0, NEGS - 1 if k == 0 else NEGS)], row_ssem.at[k])
    settle(emb_all.at[pl.ds(0, NEGS - 1)], emb_sem.at[0])
    settle(sc_all.at[pl.ds(0, NEGS - 1)], sc_sem.at[0])
    settle(eg_send.at[pl.ds(0, NEGS - 1)], eg_sem.at[0])
    for t, (low, high) in enumerate(COLS):
        settle(p_send.at[:, pl.ds(low, high - low)], p_ssem.at[t])
        for stage in range(3):
            settle(
                stages[stage][0].at[t, pl.ds(0, YS - 1), :, pl.ds(0, high - low)],
                s_ssem.at[stage, t],
            )


def local(
    feature_table, cur_rows, next_owner, next_local, slot_counts, hop_counts, positive_ids,
    neighbor_weight, combine_weight, candidates,
):
    vmem = pl.BlockSpec(memory_space=pltpu.VMEM)
    smem = pl.BlockSpec(memory_space=pltpu.SMEM)
    hbm = pl.BlockSpec(memory_space=pl.ANY)
    dma = pltpu.SemaphoreType.DMA
    part = H // 4
    scratch = [
        pltpu.VMEM((REQ, F), BF16),
        pltpu.VMEM((3, 2, 512, REQ), BF16),
        pltpu.VMEM((F, F), BF16),
        pltpu.VMEM((TILES, F, TILE), BF16),
        pltpu.VMEM((TILES, F + H, TILE), BF16),
        pltpu.VMEM((2 * OWN, H), BF16),
        pltpu.VMEM((REQ, H), BF16),
        pltpu.VMEM((2, REQ, 768), BF16),
        pltpu.VMEM((HOP1, F + H), BF16),
        pltpu.VMEM((HOP1, H), F32),
        pltpu.VMEM((HOP1, H), F32),
        pltpu.VMEM((REPS, NEGS, 1, 128), F32),
        pltpu.VMEM((REPS, NEGS, 1, 128), F32),
        pltpu.VMEM((REPS, NEGS, 1, 128), F32),
        pltpu.VMEM((DEVS, 128), F32),
        pltpu.VMEM((YS, NEGS, 16, WIDE), BF16),
        pltpu.VMEM((YS, NEGS, CORES, 16, WIDE), BF16),
        pltpu.VMEM((YS, NEGS, CORES, 16, WIDE), BF16),
        pltpu.VMEM((REQ, 16), F32),
        pltpu.VMEM((16, part), BF16),
        pltpu.VMEM((NEGS, 16, part), BF16),
        pltpu.VMEM((64, H), BF16),
        pltpu.VMEM((32, 128), F32),
        pltpu.VMEM((NEGS, 32, 128), F32),
        pltpu.VMEM((NEGS, 16, part), BF16),
        pltpu.VMEM((NEGS, 16, part), BF16),
        pltpu.VMEM((512, H), BF16),
        pltpu.VMEM((512, H), BF16),
        pltpu.VMEM((2, 512, 768), F32),
        pltpu.VMEM((3, YS, 128, 768), BF16),
        pltpu.VMEM((3, YS, 128, 768), BF16),
        pltpu.VMEM((3, YS, 32, 768), BF16),
        pltpu.VMEM((3, YS, 32, 768), BF16),
        pltpu.VMEM((3, YS, 8, 768), F32),
        pltpu.VMEM((3, YS, 8, 768), F32),
        dma((4 + 2 * TILES,)),
        dma((4,)), dma((YS,)), dma((YS,)), dma((YS,)), dma((YS,)),
        dma((2,)), dma((2,)), dma((2,)),
        dma((3,)), dma((3,)),
        dma((3, 3)), dma((3, 3)),
    ]
    next_rows, loss, cand_grad, neighbor_grad = pl.pallas_call(
        kernel,
        out_shape=(
            pltpu.VMEM((REQ, F), BF16),
            pltpu.VMEM((1, B), F32),
            pltpu.VMEM((OWN, H), F32),
            pltpu.VMEM((8, H), F32),
        ),
        in_specs=[vmem, vmem, vmem, vmem, smem, hbm, hbm, hbm, hbm, hbm],
        out_specs=(vmem, vmem, vmem, vmem),
        scratch_shapes=scratch,
        compiler_params=pltpu.CompilerParams(
            collective_id=0, has_side_effects=True, vmem_limit_bytes=60 * 2**20
        ),
        name="step",
    )(
        next_owner.reshape(1, REQ),
        next_local,
        slot_counts.T,
        hop_counts,
        positive_ids,
        feature_table,
        cur_rows,
        neighbor_weight,
        combine_weight,
        candidates,
    )
    return next_rows, loss.reshape(B), cand_grad, neighbor_grad


def solution(mesh):
    both = P(("rep", "neg"), None)
    flat = P(("rep", "neg"))
    return jax.shard_map(
        local,
        mesh=mesh,
        in_specs=(both, both, both, flat, both, both, flat, P(), P(), both),
        out_specs=(both, flat, both, both),
        check_vma=False,
    )
```

```python
import jax
import jax.numpy as jnp
from jax import lax
from jax.experimental import pallas as pl
from jax.experimental.pallas import tpu as pltpu
from jax.sharding import PartitionSpec as P

EPSILON = 1e-06
MARGIN = 0.5
MESH = pl.DeviceIdType.MESH
F32 = jnp.float32
BF16 = jnp.bfloat16
HIGH = lax.Precision.HIGHEST

REPS, NEGS, DEVS = 8, 16, 128
YS, CORES = 4, 2
F, H = 1024, 2048
TILE = 512
TILES = H // TILE
REQ, HOP1, SLOTS, B, K1 = 768, 48, 16, 4, 12
PART = 256
WIDE = 3 * PART
OWN = 64
STOPS = (16, 26, 38, 50, 58, 64, 64, 64)


def iota(shape, dim):
    return lax.broadcasted_iota(jnp.int32, shape, dim)


def nt(a, b, precision=None):
    return lax.dot_general(
        a, b, (((1,), (1,)), ((), ())), preferred_element_type=F32, precision=precision
    )


def tn(a, b, precision=None):
    return lax.dot_general(
        a, b, (((0,), (0,)), ((), ())), preferred_element_type=F32, precision=precision
    )


def nn(a, b, precision=None):
    return jnp.dot(a, b, preferred_element_type=F32, precision=precision)


def bf(mask):
    return mask.astype(F32).astype(BF16)


def kernel(
    owner_ref, local_ref, slot_ref, hop_ref, pos_ref,
    table_hbm, cur_hbm, nw_hbm, cw_hbm, cand_hbm,
    rows_acc, loss_ref, cand_out, ngrad_ref,
    cur_v, curt_v, table_v, nw_v, cw_v, cand_v, mask_v, pgrad_v, x_v, mixed_v, pooled_g,
    ask_send, ask_mid, ask_recv, ids_v, row_out, row_send, row_recv, cols_v,
    emb_send, emb_all, e_v, sc_send, sc_all, eg_send, eg_recv,
    p_send, p_recv, p_own, a1_send, a1_recv, a2_f, a2_send, a2_recv,
    b1_f, b1_send, b1_recv, b2_f, b2_send, b2_recv,
    in_sem, ask_sem, out_ssem, out_rsem, row_ssem, row_rsem,
    emb_sem, sc_sem, eg_sem, p_ssem, p_rsem, a1_ssem, a1_rsem, a2_sem, b1_ssem, b1_rsem, b2_sem,
):
    rep = lax.axis_index("rep")
    neg = lax.axis_index("neg")
    y, core = rep // CORES, lax.rem(rep, CORES)
    x, z = neg // 4, lax.rem(neg, 4)
    mate = (y * CORES + 1 - core, neg)

    def send(src, dst, ssem, rsem, where):
        pltpu.make_async_remote_copy(
            src_ref=src, dst_ref=dst, send_sem=ssem, recv_sem=rsem,
            device_id=where, device_id_type=MESH,
        ).start()

    def settle(ref, sem):
        pltpu.make_async_copy(ref, ref, sem).wait()

    def around(here, count, body):
        def step(i, carry):
            body(lax.rem(here + i, count))
            return carry

        lax.fori_loop(1, count, step, 0)

    barrier = pltpu.get_barrier_semaphore()

    def greet(where):
        pl.semaphore_signal(barrier, inc=1, device_id=where, device_id_type=MESH)

    around(neg, NEGS, lambda n: greet((rep, n)))
    around(rep, REPS, lambda r: greet((r, neg)))

    loads = [
        pltpu.make_async_copy(cur_hbm, cur_v, in_sem.at[0]),
        pltpu.make_async_copy(table_hbm, table_v, in_sem.at[1]),
        pltpu.make_async_copy(cand_hbm, cand_v.at[pl.ds(0, OWN)], in_sem.at[2]),
        pltpu.make_async_copy(cand_hbm, cand_v.at[pl.ds(OWN, OWN)], in_sem.at[3]),
    ]
    nw_loads = [
        pltpu.make_async_copy(
            nw_hbm.at[:, pl.ds(j * TILE, TILE)], nw_v.at[j], in_sem.at[4 + j]
        )
        for j in range(TILES)
    ]
    cw_loads = [
        pltpu.make_async_copy(
            cw_hbm.at[:, pl.ds(j * TILE, TILE)], cw_v.at[j], in_sem.at[4 + TILES + j]
        )
        for j in range(TILES)
    ]
    loads[0].start()
    for load in nw_loads:
        load.start()

    owner = owner_ref[...]
    hit = owner == iota((DEVS, REQ), 0)
    hit_low = bf(hit)
    before = bf(iota((REQ, REQ), 0) < iota((REQ, REQ), 1))
    count = nn(hit_low, before)
    rank = jnp.sum(jnp.where(hit, count, 0.0), axis=0, keepdims=True)
    local = local_ref[...].reshape(1, REQ)
    line = iota((DEVS, REQ), 0).astype(F32)
    pay = jnp.where(line == rank, (local >> 5).astype(F32), 0.0) + jnp.where(
        line == rank + 16.0, (local & 31).astype(F32), 0.0
    )
    asks = nt(hit_low, pay.astype(BF16))
    lane1 = iota((1, 128), 1)
    positives = jnp.zeros((1, 128), jnp.int32)
    for t in range(B):
        value = pos_ref[t]
        positives = positives + jnp.where(lane1 == 32 + t, value >> 5, 0)
        positives = positives + jnp.where(lane1 == 36 + t, value & 31, 0)
    asks = asks + positives.astype(F32)
    ask_send[...] = asks.reshape(REPS, NEGS, 1, 128)

    pl.semaphore_wait(barrier, NEGS - 1 + REPS - 1)
    around(
        rep, REPS,
        lambda r: send(
            ask_send.at[r], ask_mid.at[rep], ask_sem.at[0], ask_sem.at[1], (r, neg)
        ),
    )
    ask_mid[rep] = ask_send[rep]
    for load in loads[1:]:
        load.start()
    for load in cw_loads:
        load.start()

    from_x = (x + 4 - ((owner >> 2) & 3)) & 3
    from_z = (z + 4 - (owner & 3)) & 3
    from_y = (y + 4 - (owner >> 5)) & 3
    turn = (from_x + from_y + from_z) & 3
    placed = turn * 32 + (from_x * 4 + from_z) * 2 + ((owner >> 4) & 1)
    eye = bf(iota((REQ, REQ), 0) == iota((REQ, REQ), 1))
    pair = jnp.where(iota((16, REQ), 0) == 0, placed.astype(F32), rank).astype(BF16)
    cols_v[...] = nt(eye, pair)

    spread = bf(iota((REQ, HOP1), 0) // SLOTS == iota((REQ, HOP1), 1))
    counts = nt(spread, slot_ref[...].astype(F32).astype(BF16))
    at_slot = iota((REQ, SLOTS), 0) % SLOTS == iota((REQ, SLOTS), 1)
    weight = jnp.sum(jnp.where(at_slot, counts, 0.0), axis=1, keepdims=True) / jnp.sum(
        counts, axis=1, keepdims=True
    )

    loads[0].wait()

    def project(j):
        nw_loads[j].wait()
        projected = nn(cur_v[...], nw_v[j])
        mask_v[j] = bf(projected > 0.0)
        weighted = jnp.maximum(projected, 0.0) * weight
        pooled = jnp.sum(weighted.reshape(HOP1, SLOTS, TILE), axis=1)
        x_v[:, F + j * TILE : F + (j + 1) * TILE] = pooled.astype(BF16)

    settle(ask_mid.at[pl.ds(0, REPS - 1)], ask_sem.at[1])
    around(
        neg, NEGS,
        lambda n: send(
            ask_mid.at[:, n], ask_recv.at[:, neg], ask_sem.at[2], ask_sem.at[3], (rep, n)
        ),
    )
    ask_recv[:, neg] = ask_mid[:, neg]
    for j in range(TILES // 2):
        project(j)
    loads[1].wait()
    settle(ask_recv.at[:, pl.ds(0, NEGS - 1)], ask_sem.at[3])
    line_i, line_d = iota((DEVS, DEVS), 0), iota((DEVS, DEVS), 1)
    to_x, to_z = (line_i >> 2) & 3, line_i & 3
    to_y = (y + 8 + (line_i >> 5) - to_x - to_z) & 3
    target = to_y * 32 + ((line_i >> 4) & 1) * 16 + ((x + to_x) & 3) * 4 + ((z + to_z) & 3)
    ids_v[...] = nn(bf(target == line_d), ask_recv[...].reshape(DEVS, 128).astype(BF16))

    def serve(k):
        first_half = pl.multiple_of(k * 32 + (1 - core) * NEGS, NEGS)
        second_half = pl.multiple_of(k * 32 + core * NEGS, NEGS)
        asked = jnp.concatenate(
            [ids_v[pl.ds(first_half, NEGS), :], ids_v[pl.ds(second_half, NEGS), :]], axis=0
        ).astype(BF16)

        def chosen(rows, per, slot_of):
            wide = nn(bf(iota((rows, 32), 0) // per % 32 == iota((rows, 32), 1)), asked)
            slot = slot_of(iota((rows, 1), 0))
            at = iota((rows, 128), 1)
            ids = jnp.sum(
                jnp.where(at == slot, wide * 32.0, 0.0) + jnp.where(at == slot + 16, wide, 0.0),
                axis=1,
                keepdims=True,
            )
            return bf(ids == iota((rows, F), 1).astype(F32))

        main = nn(chosen(512, 16, lambda r: r % 16), table_v[:, 0:WIDE]).reshape(32, 16, WIDE)
        tail = nn(
            chosen(768, 8, lambda r: jnp.maximum(r % 8 - 4, 0) * 3 + r // 256),
            table_v[:, WIDE:F],
        )
        high = iota((32, 8, PART), 1) >= 4
        parts = []
        for c in range(3):
            own = main[:, 8:16, c * PART : (c + 1) * PART]
            parts.append(
                jnp.where(high, tail[256 * c : 256 * (c + 1)].reshape(32, 8, PART), own)
            )
        lower = jnp.concatenate(parts, axis=2)
        block = jnp.concatenate([main[:, 0:8, :], lower], axis=1).astype(BF16)
        row_out[k] = block[0:NEGS]
        send(row_out.at[k], row_send.at[k, :, core], out_ssem.at[k], out_rsem.at[k], mate)
        row_send[k, :, core] = block[NEGS:32]

    done = {"sent": 0, "served": 0}

    def serve_to(rounds):
        while done["served"] < rounds:
            serve(done["served"])
            done["served"] += 1

    def post_to(limit, rounds=0):
        while done["sent"] < limit:
            k = done["sent"] // NEGS
            serve_to(k + 1)
            low, high = done["sent"] - k * NEGS, min(limit - k * NEGS, NEGS)
            done["sent"] = k * NEGS + high

            def one(i, carry):
                j = lax.rem(i + core * (NEGS - 2 * i), NEGS)
                dx, dz = j // 4, lax.rem(j, 4)
                dy = lax.rem(k + 8 - dx - dz, YS)
                where = (
                    lax.rem(y + dy, YS) * CORES + core,
                    lax.rem(x + dx, 4) * 4 + lax.rem(z + dz, 4),
                )
                send(
                    row_send.at[k, j], row_recv.at[k, j], row_ssem.at[k], row_rsem.at[k], where
                )
                return carry

            if low == 0:
                settle(row_out.at[k], out_rsem.at[k])
                if k == 0:
                    row_recv[0, 0] = row_send[0, 0]
                    low = 1
            lax.fori_loop(low, high, one, 0)
        serve_to(rounds)

    post_to(STOPS[0], 1)
    for j in range(TILES // 2, TILES):
        project(j)
    first = bf(iota((HOP1, REQ), 0) * SLOTS == iota((HOP1, REQ), 1))
    x_v[:, 0:F] = nn(first, cur_v[...]).astype(BF16)

    pooled_x = x_v[...]
    for j in range(TILES):
        cw_loads[j].wait()
        mixed_v[:, j * TILE : (j + 1) * TILE] = nn(pooled_x, cw_v[j])
    mixed_in = mixed_v[...]
    mixed = jnp.maximum(mixed_in, 0.0)
    inv_mid = lax.rsqrt(jnp.mean(mixed * mixed, axis=1, keepdims=True) + EPSILON)
    normed = mixed * inv_mid
    top_rows = bf(iota((8, B), 0) == iota((8, B), 1))
    hops = nn(top_rows, hop_ref[...].astype(F32).astype(BF16))
    lanes_of = bf(iota((K1, HOP1), 0) == iota((K1, HOP1), 1) % K1)
    own_hop = iota((8, HOP1), 0) == iota((8, HOP1), 1) // K1
    hop_total = jnp.maximum(jnp.sum(hops, axis=1, keepdims=True), 1.0)
    hop_mat = jnp.where(own_hop, nn(hops.astype(BF16), lanes_of), 0.0) / hop_total
    top_in = nn(hop_mat, normed, HIGH)
    inv_top = lax.rsqrt(jnp.mean(top_in * top_in, axis=1, keepdims=True) + EPSILON)
    embedding = (top_in * inv_top).astype(BF16)
    part = H // 4
    packed = jnp.zeros((16, part), F32)
    for c in range(4):
        move = bf(
            (iota((16, 8), 0) == iota((16, 8), 1) + 4 * c) & (iota((16, 8), 1) < B)
        )
        packed = packed + nn(move, embedding[:, c * part : (c + 1) * part])
    emb_send[...] = packed.astype(BF16)
    around(
        neg, NEGS,
        lambda n: send(emb_send, emb_all.at[neg], emb_sem.at[0], emb_sem.at[1], (rep, n)),
    )
    emb_all[neg] = emb_send[...]

    post_to(STOPS[1], 2)
    loads[2].wait()
    loads[3].wait()
    settle(emb_all.at[pl.ds(0, NEGS - 1)], emb_sem.at[1])

    gathered = emb_all[...].reshape(256, part)
    row_q, col_q = iota((64, 256), 0), iota((64, 256), 1)
    for c in range(4):
        move = bf(col_q == (row_q // 4) * 16 + 4 * c + row_q % 4)
        e_v[:, c * part : (c + 1) * part] = nn(move, gathered).astype(BF16)
    left = iota((32, 128), 1) < OWN
    scores = jnp.where(left, nt(e_v[0:32, :], cand_v[...]), nt(e_v[32:64, :], cand_v[...]))
    sc_send[...] = scores
    around(
        neg, NEGS,
        lambda n: send(sc_send, sc_all.at[neg], sc_sem.at[0], sc_sem.at[1], (rep, n)),
    )
    sc_all[neg] = scores

    post_to(STOPS[2], 3)
    mates = ask_recv[rep].reshape(NEGS, 128).astype(BF16)
    halves = []
    for h in range(2):
        pick = bf(iota((32, NEGS), 0) // B + 8 * h == iota((32, NEGS), 1))
        wide = nn(pick, mates)
        at, t = iota((32, 128), 1), iota((32, 128), 0) % B
        halves.append(
            jnp.sum(
                jnp.where(at == 32 + t, wide * 32.0, 0.0) + jnp.where(at == 36 + t, wide, 0.0),
                axis=1,
                keepdims=True,
            )
        )
    positive = jnp.where(left, halves[0], halves[1])
    settle(sc_all.at[pl.ds(0, NEGS - 1)], sc_sem.at[1])

    def by_half(values):
        first = jnp.sum(jnp.where(left, values, 0.0), axis=1, keepdims=True)
        second = jnp.sum(jnp.where(left, 0.0, values), axis=1, keepdims=True)
        return jnp.where(left, first, second)

    all_scores = sc_all[...]
    shape = (NEGS, 32, 128)
    cand_id = (iota(shape, 0) * OWN + iota(shape, 2) % OWN).astype(F32)
    is_pos = cand_id == positive[None]
    pos_score = by_half(jnp.sum(jnp.where(is_pos, all_scores, 0.0), axis=0))
    gaps = all_scores - pos_score[None] + MARGIN
    small = jnp.exp(-jnp.abs(gaps))
    losses = jnp.maximum(gaps, 0.0) + jnp.log1p(small)
    sigmoid = jnp.where(gaps >= 0.0, 1.0, small) / (1.0 + small)
    loss = by_half(jnp.sum(losses, axis=0)) / (NEGS * OWN)
    totals = by_half(jnp.sum(sigmoid, axis=0))
    own_gap = sc_all[neg] - pos_score + MARGIN
    own_small = jnp.exp(-jnp.abs(own_gap))
    own_sig = jnp.where(own_gap >= 0.0, 1.0, own_small) / (1.0 + own_small)
    own_id = (neg * OWN + iota((32, 128), 1) % OWN).astype(F32)
    score_grad = (own_sig - jnp.where(own_id == positive, totals, 0.0)) / (NEGS * OWN)

    g_left = jnp.where(left, score_grad, 0.0).astype(BF16)
    g_right = jnp.where(left, 0.0, score_grad).astype(BF16)
    eg = jnp.concatenate([nn(g_left, cand_v[...]), nn(g_right, cand_v[...])], axis=0).astype(BF16)
    row_p, col_p = iota((256, 64), 0), iota((256, 64), 1)
    eg_out = jnp.zeros((256, part), F32)
    for c in range(4):
        move = bf((row_p // 16 == col_p // 4) & (row_p % 16 == 4 * c + col_p % 4))
        eg_out = eg_out + nn(move, eg[:, c * part : (c + 1) * part])
    eg_send[...] = eg_out.astype(BF16).reshape(NEGS, 16, part)
    around(
        neg, NEGS,
        lambda n: send(eg_send.at[n], eg_recv.at[neg], eg_sem.at[0], eg_sem.at[1], (rep, n)),
    )
    eg_recv[neg] = eg_send[neg]

    post_to(STOPS[3], 4)
    for b in range(8):
        curt_v[b % 2, 128 * (b // 2) : 128 * (b // 2) + 128, :] = (
            cur_v[:, 128 * b : 128 * b + 128].astype(F32).T.astype(BF16)
        )
    settle(eg_recv.at[pl.ds(0, NEGS - 1)], eg_sem.at[1])
    eg_sum = jnp.sum(eg_recv[...].astype(F32), axis=0)
    embed_grad = []
    for c in range(4):
        move = (
            (iota((8, 16), 1) == iota((8, 16), 0) + 4 * c) & (iota((8, 16), 0) < B)
        ).astype(F32)
        embed_grad.append(nn(move, eg_sum, HIGH))
    embed_grad = jnp.concatenate(embed_grad, axis=1)

    post_to(STOPS[4])

    top_grad = inv_top * embed_grad - top_in * (
        inv_top * inv_top * inv_top * jnp.mean(embed_grad * top_in, axis=1, keepdims=True)
    )
    normed_grad = tn(hop_mat, top_grad, HIGH)
    mixed_grad = inv_mid * normed_grad - mixed * (
        inv_mid * inv_mid * inv_mid * jnp.mean(normed_grad * mixed, axis=1, keepdims=True)
    )
    mixed_in_grad = jnp.where(mixed_in > 0.0, mixed_grad, 0.0).astype(BF16)
    total = jnp.zeros((HOP1, H), F32)
    for j in range(TILES):
        total = total + nt(mixed_in_grad[:, j * TILE : (j + 1) * TILE], cw_v[j, F : F + H, :])
    pooled_g[...] = total

    post_to(STOPS[5])

    def products(j, slot):
        spread_grad = jnp.broadcast_to(
            pooled_g[:, j * TILE : (j + 1) * TILE][:, None, :], (HOP1, SLOTS, TILE)
        ).reshape(REQ, TILE)
        pgrad_v[slot] = jnp.where(
            mask_v[j].astype(F32) > 0.0, spread_grad * weight, 0.0
        ).astype(BF16)
        p_send[j] = nn(curt_v[1 - core], pgrad_v[slot]).astype(BF16)
        send(p_send.at[j], p_recv.at[j], p_ssem.at[j], p_rsem.at[j], mate)
        p_own[j] = nn(curt_v[core], pgrad_v[slot])

    def pass_on(j):
        settle(p_recv.at[j], p_rsem.at[j])
        chip_sum = p_own[j] + p_recv[j].astype(F32)
        if j < 2:
            a1_send[j] = chip_sum.astype(BF16).reshape(YS, 128, TILE)
            around(
                y, YS,
                lambda q: send(
                    a1_send.at[j, q], a1_recv.at[j, y], a1_ssem.at[j], a1_rsem.at[j],
                    (q * CORES + core, neg),
                ),
            )
            a1_recv[j, y] = a1_send[j, y]
        else:
            k = j - 2
            for q in range(YS):
                b1_f[:, 8 * q : 8 * q + 8, :] = chip_sum[128 * q : 128 * q + 128].reshape(
                    NEGS, 8, TILE
                )
            b1_send[k] = b1_f[...].astype(BF16)
            around(
                neg, NEGS,
                lambda n: send(
                    b1_send.at[k, n], b1_recv.at[k, neg], b1_ssem.at[k], b1_rsem.at[k], (rep, n)
                ),
            )
            b1_recv[k, neg] = b1_send[k, neg]

    order = (0, 2, 1, 3)
    for step, j in enumerate(order):
        products(j, step % 2)
        if step > 0:
            pass_on(order[step - 1])
    pass_on(order[-1])
    post_to(STOPS[6])

    owner_col = cols_v[:, 0:1]
    rank_col = cols_v[:, 1:2]
    third = jnp.floor((rank_col + 0.5) * (1.0 / 3.0))
    left_over = rank_col - 3.0 * third
    slot_main = owner_col * 16.0 + rank_col
    slot_tail = [
        jnp.where(left_over == float(c), owner_col * 16.0 + 12.0 + third, -1.0) for c in range(3)
    ]

    def place(k):
        settle(row_recv.at[k, pl.ds(0, NEGS - 1 if k == 0 else NEGS)], row_rsem.at[k])
        block = row_recv[k].reshape(512, WIDE)
        line = (iota((REQ, 512), 1) + k * 512).astype(F32)
        body = nn(bf(line == slot_main), block)
        tail = jnp.zeros((REQ, PART), F32)
        for c in range(3):
            tail = tail + nn(bf(line == slot_tail[c]), block[:, c * PART : (c + 1) * PART])
        new = jnp.concatenate([body, tail], axis=1).astype(BF16)
        rows_acc[...] = new if k == 0 else rows_acc[...] + new

    lines = (iota((32, 128), 0) == iota((32, 128), 1) + B * (neg % 8)).astype(F32)
    half = jnp.where(neg // 8 == 0, 0, OWN)
    mine = tn(loss, lines, HIGH)
    loss_ref[...] = jnp.sum(
        jnp.where(iota((128, 128), 0) == half, mine, 0.0), axis=0, keepdims=True
    )[:, 0:B]
    cand_out[...] = tn(g_left, e_v[0:32, :])[0:OWN] + tn(g_right, e_v[32:64, :])[OWN:128]
    place(0)
    place(1)
    place(2)

    for j in range(2):
        settle(a1_recv.at[j, pl.ds(0, YS - 1)], a1_rsem.at[j])
        a2_f[:, 8 * j : 8 * j + 8, :] = jnp.sum(a1_recv[j].astype(F32), axis=0).reshape(
            NEGS, 8, TILE
        )
    a2_send[...] = a2_f[...].astype(BF16)
    around(
        neg, NEGS,
        lambda n: send(a2_send.at[n], a2_recv.at[neg], a2_sem.at[0], a2_sem.at[1], (rep, n)),
    )
    a2_recv[neg] = a2_send[neg]
    for k in range(2):
        settle(b1_recv.at[k, pl.ds(0, NEGS - 1)], b1_rsem.at[k])
        b2_f[:, 8 * k : 8 * k + 8, :] = jnp.sum(b1_recv[k].astype(F32), axis=0).reshape(
            YS, 8, TILE
        )
    b2_send[...] = b2_f[...].astype(BF16)
    around(
        y, YS,
        lambda q: send(
            b2_send.at[q], b2_recv.at[y], b2_sem.at[0], b2_sem.at[1], (q * CORES + core, neg)
        ),
    )
    b2_recv[y] = b2_send[y]

    post_to(STOPS[7])
    place(3)

    settle(a2_recv.at[pl.ds(0, NEGS - 1)], a2_sem.at[1])
    a_sum = jnp.sum(a2_recv[...].astype(F32), axis=0)
    settle(b2_recv.at[pl.ds(0, YS - 1)], b2_sem.at[1])
    b_sum = jnp.sum(b2_recv[...].astype(F32), axis=0)
    for j in range(2):
        ngrad_ref[:, j * TILE : (j + 1) * TILE] = a_sum[8 * j : 8 * j + 8]
        ngrad_ref[:, (j + 2) * TILE : (j + 3) * TILE] = b_sum[8 * j : 8 * j + 8]

    settle(ask_send.at[pl.ds(0, REPS - 1)], ask_sem.at[0])
    settle(ask_mid.at[:, pl.ds(0, NEGS - 1)], ask_sem.at[2])
    for k in range(YS):
        settle(row_out.at[k], out_ssem.at[k])
        settle(row_send.at[k, pl.ds(0, NEGS - 1 if k == 0 else NEGS)], row_ssem.at[k])
    settle(emb_all.at[pl.ds(0, NEGS - 1)], emb_sem.at[0])
    settle(sc_all.at[pl.ds(0, NEGS - 1)], sc_sem.at[0])
    settle(eg_send.at[pl.ds(0, NEGS - 1)], eg_sem.at[0])
    for j in range(TILES):
        settle(p_send.at[j], p_ssem.at[j])
    for j in range(2):
        settle(a1_send.at[j, pl.ds(0, YS - 1)], a1_ssem.at[j])
        settle(b1_send.at[j, pl.ds(0, NEGS - 1)], b1_ssem.at[j])
    settle(a2_send.at[pl.ds(0, NEGS - 1)], a2_sem.at[0])
    settle(b2_send.at[pl.ds(0, YS - 1)], b2_sem.at[0])


def local(
    feature_table, cur_rows, next_owner, next_local, slot_counts, hop_counts, positive_ids,
    neighbor_weight, combine_weight, candidates,
):
    vmem = pl.BlockSpec(memory_space=pltpu.VMEM)
    smem = pl.BlockSpec(memory_space=pltpu.SMEM)
    hbm = pl.BlockSpec(memory_space=pl.ANY)
    dma = pltpu.SemaphoreType.DMA
    part = H // 4
    scratch = [
        pltpu.VMEM((REQ, F), BF16),
        pltpu.VMEM((2, 512, REQ), BF16),
        pltpu.VMEM((F, F), BF16),
        pltpu.VMEM((TILES, F, TILE), BF16),
        pltpu.VMEM((TILES, F + H, TILE), BF16),
        pltpu.VMEM((2 * OWN, H), BF16),
        pltpu.VMEM((TILES, REQ, TILE), BF16),
        pltpu.VMEM((2, REQ, TILE), BF16),
        pltpu.VMEM((HOP1, F + H), BF16),
        pltpu.VMEM((HOP1, H), F32),
        pltpu.VMEM((HOP1, H), F32),
        pltpu.VMEM((REPS, NEGS, 1, 128), F32),
        pltpu.VMEM((REPS, NEGS, 1, 128), F32),
        pltpu.VMEM((REPS, NEGS, 1, 128), F32),
        pltpu.VMEM((DEVS, 128), F32),
        pltpu.VMEM((YS, NEGS, 16, WIDE), BF16),
        pltpu.VMEM((YS, NEGS, CORES, 16, WIDE), BF16),
        pltpu.VMEM((YS, NEGS, CORES, 16, WIDE), BF16),
        pltpu.VMEM((REQ, 16), F32),
        pltpu.VMEM((16, part), BF16),
        pltpu.VMEM((NEGS, 16, part), BF16),
        pltpu.VMEM((64, H), BF16),
        pltpu.VMEM((32, 128), F32),
        pltpu.VMEM((NEGS, 32, 128), F32),
        pltpu.VMEM((NEGS, 16, part), BF16),
        pltpu.VMEM((NEGS, 16, part), BF16),
        pltpu.VMEM((TILES, 512, TILE), BF16),
        pltpu.VMEM((TILES, 512, TILE), BF16),
        pltpu.VMEM((TILES, 512, TILE), F32),
        pltpu.VMEM((2, YS, 128, TILE), BF16),
        pltpu.VMEM((2, YS, 128, TILE), BF16),
        pltpu.VMEM((NEGS, 16, TILE), F32),
        pltpu.VMEM((NEGS, 16, TILE), BF16),
        pltpu.VMEM((NEGS, 16, TILE), BF16),
        pltpu.VMEM((NEGS, 32, TILE), F32),
        pltpu.VMEM((2, NEGS, 32, TILE), BF16),
        pltpu.VMEM((2, NEGS, 32, TILE), BF16),
        pltpu.VMEM((YS, 16, TILE), F32),
        pltpu.VMEM((YS, 16, TILE), BF16),
        pltpu.VMEM((YS, 16, TILE), BF16),
        dma((4 + 2 * TILES,)),
        dma((4,)), dma((YS,)), dma((YS,)), dma((YS,)), dma((YS,)),
        dma((2,)), dma((2,)), dma((2,)),
        dma((TILES,)), dma((TILES,)),
        dma((2,)), dma((2,)), dma((2,)),
        dma((2,)), dma((2,)), dma((2,)),
    ]
    next_rows, loss, cand_grad, neighbor_grad = pl.pallas_call(
        kernel,
        out_shape=(
            pltpu.VMEM((REQ, F), BF16),
            pltpu.VMEM((1, B), F32),
            pltpu.VMEM((OWN, H), F32),
            pltpu.VMEM((8, H), F32),
        ),
        in_specs=[vmem, vmem, vmem, vmem, smem, hbm, hbm, hbm, hbm, hbm],
        out_specs=(vmem, vmem, vmem, vmem),
        scratch_shapes=scratch,
        compiler_params=pltpu.CompilerParams(
            collective_id=0, has_side_effects=True, vmem_limit_bytes=58 * 2**20
        ),
        name="step",
    )(
        next_owner.reshape(1, REQ),
        next_local,
        slot_counts.T,
        hop_counts,
        positive_ids,
        feature_table,
        cur_rows,
        neighbor_weight,
        combine_weight,
        candidates,
    )
    return next_rows, loss.reshape(B), cand_grad, neighbor_grad


def solution(mesh):
    both = P(("rep", "neg"), None)
    flat = P(("rep", "neg"))
    return jax.shard_map(
        local,
        mesh=mesh,
        in_specs=(both, both, both, flat, both, both, flat, P(), P(), both),
        out_specs=(both, flat, both, both),
        check_vma=False,
    )
```

```python
import jax
import jax.numpy as jnp
from jax import lax
from jax.experimental import pallas as pl
from jax.experimental.pallas import tpu as pltpu
from jax.sharding import PartitionSpec as P

EPSILON = 1e-06
MARGIN = 0.5
MESH = pl.DeviceIdType.MESH
F32 = jnp.float32
BF16 = jnp.bfloat16
HIGH = lax.Precision.HIGHEST

REPS, NEGS, DEVS = 8, 16, 128
YS, CORES = 4, 2
F, H = 1024, 2048
TILE = 512
TILES = H // TILE
REQ, HOP1, SLOTS, B, K1 = 768, 48, 16, 4, 12
PART = 256
WIDE = 3 * PART
OWN = 64
STOPS = (16, 26, 38, 50, 64, 64, 64, 64)


def iota(shape, dim):
    return lax.broadcasted_iota(jnp.int32, shape, dim)


def nt(a, b, precision=None):
    return lax.dot_general(
        a, b, (((1,), (1,)), ((), ())), preferred_element_type=F32, precision=precision
    )


def tn(a, b, precision=None):
    return lax.dot_general(
        a, b, (((0,), (0,)), ((), ())), preferred_element_type=F32, precision=precision
    )


def nn(a, b, precision=None):
    return jnp.dot(a, b, preferred_element_type=F32, precision=precision)


def bf(mask):
    return mask.astype(F32).astype(BF16)


def kernel(
    owner_ref, local_ref, slot_ref, hop_ref, pos_ref,
    table_hbm, cur_hbm, nw_hbm, cw_hbm, cand_hbm,
    rows_acc, loss_ref, cand_out, ngrad_ref,
    cur_v, curt_v, table_v, nw_v, cw_v, cand_v, mask_v, pgrad_v, x_v, mixed_v, pooled_g,
    ask_send, ask_mid, ask_recv, ids_v, row_out, row_send, row_recv, cols_v,
    emb_send, emb_all, e_v, sc_send, sc_all, eg_send, eg_recv,
    p_send, p_recv, p_own, a1_send, a1_recv, a2_f, a2_send, a2_recv,
    b1_f, b1_send, b1_recv, b2_f, b2_send, b2_recv,
    in_sem, ask_sem, out_ssem, out_rsem, row_ssem, row_rsem,
    emb_sem, sc_sem, eg_sem, p_ssem, p_rsem, a1_ssem, a1_rsem, a2_sem, b1_ssem, b1_rsem, b2_sem,
):
    rep = lax.axis_index("rep")
    neg = lax.axis_index("neg")
    y, core = rep // CORES, lax.rem(rep, CORES)
    x, z = neg // 4, lax.rem(neg, 4)
    mate = (y * CORES + 1 - core, neg)

    def send(src, dst, ssem, rsem, where):
        pltpu.make_async_remote_copy(
            src_ref=src, dst_ref=dst, send_sem=ssem, recv_sem=rsem,
            device_id=where, device_id_type=MESH,
        ).start()

    def settle(ref, sem):
        pltpu.make_async_copy(ref, ref, sem).wait()

    def around(here, count, body):
        def step(i, carry):
            body(lax.rem(here + i, count))
            return carry

        lax.fori_loop(1, count, step, 0)

    barrier = pltpu.get_barrier_semaphore()

    def greet(where):
        pl.semaphore_signal(barrier, inc=1, device_id=where, device_id_type=MESH)

    around(neg, NEGS, lambda n: greet((rep, n)))
    around(rep, REPS, lambda r: greet((r, neg)))

    loads = [
        pltpu.make_async_copy(cur_hbm, cur_v, in_sem.at[0]),
        pltpu.make_async_copy(table_hbm, table_v, in_sem.at[1]),
        pltpu.make_async_copy(cand_hbm, cand_v.at[pl.ds(0, OWN)], in_sem.at[2]),
        pltpu.make_async_copy(cand_hbm, cand_v.at[pl.ds(OWN, OWN)], in_sem.at[3]),
    ]
    nw_loads = [
        pltpu.make_async_copy(
            nw_hbm.at[:, pl.ds(j * TILE, TILE)], nw_v.at[j], in_sem.at[4 + j]
        )
        for j in range(TILES)
    ]
    cw_loads = [
        pltpu.make_async_copy(
            cw_hbm.at[:, pl.ds(j * TILE, TILE)], cw_v.at[j], in_sem.at[4 + TILES + j]
        )
        for j in range(TILES)
    ]
    loads[0].start()
    for load in nw_loads:
        load.start()

    owner = owner_ref[...]
    hit = owner == iota((DEVS, REQ), 0)
    hit_low = bf(hit)
    before = bf(iota((REQ, REQ), 0) < iota((REQ, REQ), 1))
    count = nn(hit_low, before)
    rank = jnp.sum(jnp.where(hit, count, 0.0), axis=0, keepdims=True)
    local = local_ref[...].reshape(1, REQ)
    line = iota((DEVS, REQ), 0).astype(F32)
    pay = jnp.where(line == rank, (local >> 5).astype(F32), 0.0) + jnp.where(
        line == rank + 16.0, (local & 31).astype(F32), 0.0
    )
    asks = nt(hit_low, pay.astype(BF16))
    lane1 = iota((1, 128), 1)
    positives = jnp.zeros((1, 128), jnp.int32)
    for t in range(B):
        value = pos_ref[t]
        positives = positives + jnp.where(lane1 == 32 + t, value >> 5, 0)
        positives = positives + jnp.where(lane1 == 36 + t, value & 31, 0)
    asks = asks + positives.astype(F32)
    ask_send[...] = asks.reshape(REPS, NEGS, 1, 128)

    pl.semaphore_wait(barrier, NEGS - 1 + REPS - 1)
    around(
        rep, REPS,
        lambda r: send(
            ask_send.at[r], ask_mid.at[rep], ask_sem.at[0], ask_sem.at[1], (r, neg)
        ),
    )
    ask_mid[rep] = ask_send[rep]
    for load in loads[1:]:
        load.start()
    for load in cw_loads:
        load.start()

    from_x = (x + 4 - ((owner >> 2) & 3)) & 3
    from_z = (z + 4 - (owner & 3)) & 3
    from_y = (y + 4 - (owner >> 5)) & 3
    turn = (from_x + from_y + from_z) & 3
    placed = turn * 32 + (from_x * 4 + from_z) * 2 + ((owner >> 4) & 1)
    eye = bf(iota((REQ, REQ), 0) == iota((REQ, REQ), 1))
    pair = jnp.where(iota((16, REQ), 0) == 0, placed.astype(F32), rank).astype(BF16)
    cols_v[...] = nt(eye, pair)

    spread = bf(iota((REQ, HOP1), 0) // SLOTS == iota((REQ, HOP1), 1))
    counts = nt(spread, slot_ref[...].astype(F32).astype(BF16))
    at_slot = iota((REQ, SLOTS), 0) % SLOTS == iota((REQ, SLOTS), 1)
    weight = jnp.sum(jnp.where(at_slot, counts, 0.0), axis=1, keepdims=True) / jnp.sum(
        counts, axis=1, keepdims=True
    )

    loads[0].wait()

    def project(j):
        nw_loads[j].wait()
        projected = nn(cur_v[...], nw_v[j])
        mask_v[j] = bf(projected > 0.0)
        weighted = jnp.maximum(projected, 0.0) * weight
        pooled = jnp.sum(weighted.reshape(HOP1, SLOTS, TILE), axis=1)
        x_v[:, F + j * TILE : F + (j + 1) * TILE] = pooled.astype(BF16)

    settle(ask_mid.at[pl.ds(0, REPS - 1)], ask_sem.at[1])
    around(
        neg, NEGS,
        lambda n: send(
            ask_mid.at[:, n], ask_recv.at[:, neg], ask_sem.at[2], ask_sem.at[3], (rep, n)
        ),
    )
    ask_recv[:, neg] = ask_mid[:, neg]
    for j in range(TILES // 2):
        project(j)
    loads[1].wait()
    settle(ask_recv.at[:, pl.ds(0, NEGS - 1)], ask_sem.at[3])
    line_i, line_d = iota((DEVS, DEVS), 0), iota((DEVS, DEVS), 1)
    to_x, to_z = (line_i >> 2) & 3, line_i & 3
    to_y = (y + 8 + (line_i >> 5) - to_x - to_z) & 3
    target = to_y * 32 + ((line_i >> 4) & 1) * 16 + ((x + to_x) & 3) * 4 + ((z + to_z) & 3)
    ids_v[...] = nn(bf(target == line_d), ask_recv[...].reshape(DEVS, 128).astype(BF16))

    def serve(k):
        first_half = pl.multiple_of(k * 32 + (1 - core) * NEGS, NEGS)
        second_half = pl.multiple_of(k * 32 + core * NEGS, NEGS)
        asked = jnp.concatenate(
            [ids_v[pl.ds(first_half, NEGS), :], ids_v[pl.ds(second_half, NEGS), :]], axis=0
        ).astype(BF16)

        def chosen(rows, per, slot_of):
            wide = nn(bf(iota((rows, 32), 0) // per % 32 == iota((rows, 32), 1)), asked)
            slot = slot_of(iota((rows, 1), 0))
            at = iota((rows, 128), 1)
            ids = jnp.sum(
                jnp.where(at == slot, wide * 32.0, 0.0) + jnp.where(at == slot + 16, wide, 0.0),
                axis=1,
                keepdims=True,
            )
            return bf(ids == iota((rows, F), 1).astype(F32))

        main = nn(chosen(512, 16, lambda r: r % 16), table_v[:, 0:WIDE]).reshape(32, 16, WIDE)
        tail = nn(
            chosen(768, 8, lambda r: jnp.maximum(r % 8 - 4, 0) * 3 + r // 256),
            table_v[:, WIDE:F],
        )
        high = iota((32, 8, PART), 1) >= 4
        parts = []
        for c in range(3):
            own = main[:, 8:16, c * PART : (c + 1) * PART]
            parts.append(
                jnp.where(high, tail[256 * c : 256 * (c + 1)].reshape(32, 8, PART), own)
            )
        lower = jnp.concatenate(parts, axis=2)
        block = jnp.concatenate([main[:, 0:8, :], lower], axis=1).astype(BF16)
        row_out[k] = block[0:NEGS]
        send(row_out.at[k], row_send.at[k, :, core], out_ssem.at[k], out_rsem.at[k], mate)
        row_send[k, :, core] = block[NEGS:32]

    done = {"sent": 0, "served": 0}

    def serve_to(rounds):
        while done["served"] < rounds:
            serve(done["served"])
            done["served"] += 1

    def post_to(limit, rounds=0):
        while done["sent"] < limit:
            k = done["sent"] // NEGS
            serve_to(k + 1)
            low, high = done["sent"] - k * NEGS, min(limit - k * NEGS, NEGS)
            done["sent"] = k * NEGS + high

            def one(i, carry):
                j = lax.rem(i + core * (NEGS - 2 * i), NEGS)
                dx, dz = j // 4, lax.rem(j, 4)
                dy = lax.rem(k + 8 - dx - dz, YS)
                where = (
                    lax.rem(y + dy, YS) * CORES + core,
                    lax.rem(x + dx, 4) * 4 + lax.rem(z + dz, 4),
                )
                send(
                    row_send.at[k, j], row_recv.at[k, j], row_ssem.at[k], row_rsem.at[k], where
                )
                return carry

            if low == 0:
                settle(row_out.at[k], out_rsem.at[k])
                if k == 0:
                    row_recv[0, 0] = row_send[0, 0]
                    low = 1
            lax.fori_loop(low, high, one, 0)
        serve_to(rounds)

    post_to(STOPS[0], 1)
    for j in range(TILES // 2, TILES):
        project(j)
    first = bf(iota((HOP1, REQ), 0) * SLOTS == iota((HOP1, REQ), 1))
    x_v[:, 0:F] = nn(first, cur_v[...]).astype(BF16)

    pooled_x = x_v[...]
    for j in range(TILES):
        cw_loads[j].wait()
        mixed_v[:, j * TILE : (j + 1) * TILE] = nn(pooled_x, cw_v[j])
    mixed_in = mixed_v[...]
    mixed = jnp.maximum(mixed_in, 0.0)
    inv_mid = lax.rsqrt(jnp.mean(mixed * mixed, axis=1, keepdims=True) + EPSILON)
    normed = mixed * inv_mid
    top_rows = bf(iota((8, B), 0) == iota((8, B), 1))
    hops = nn(top_rows, hop_ref[...].astype(F32).astype(BF16))
    lanes_of = bf(iota((K1, HOP1), 0) == iota((K1, HOP1), 1) % K1)
    own_hop = iota((8, HOP1), 0) == iota((8, HOP1), 1) // K1
    hop_total = jnp.maximum(jnp.sum(hops, axis=1, keepdims=True), 1.0)
    hop_mat = jnp.where(own_hop, nn(hops.astype(BF16), lanes_of), 0.0) / hop_total
    top_in = nn(hop_mat, normed, HIGH)
    inv_top = lax.rsqrt(jnp.mean(top_in * top_in, axis=1, keepdims=True) + EPSILON)
    embedding = (top_in * inv_top).astype(BF16)
    part = H // 4
    packed = jnp.zeros((16, part), F32)
    for c in range(4):
        move = bf(
            (iota((16, 8), 0) == iota((16, 8), 1) + 4 * c) & (iota((16, 8), 1) < B)
        )
        packed = packed + nn(move, embedding[:, c * part : (c + 1) * part])
    emb_send[...] = packed.astype(BF16)
    around(
        neg, NEGS,
        lambda n: send(emb_send, emb_all.at[neg], emb_sem.at[0], emb_sem.at[1], (rep, n)),
    )
    emb_all[neg] = emb_send[...]

    post_to(STOPS[1], 2)
    loads[2].wait()
    loads[3].wait()
    settle(emb_all.at[pl.ds(0, NEGS - 1)], emb_sem.at[1])

    gathered = emb_all[...].reshape(256, part)
    row_q, col_q = iota((64, 256), 0), iota((64, 256), 1)
    for c in range(4):
        move = bf(col_q == (row_q // 4) * 16 + 4 * c + row_q % 4)
        e_v[:, c * part : (c + 1) * part] = nn(move, gathered).astype(BF16)
    left = iota((32, 128), 1) < OWN
    scores = jnp.where(left, nt(e_v[0:32, :], cand_v[...]), nt(e_v[32:64, :], cand_v[...]))
    sc_send[...] = scores
    around(
        neg, NEGS,
        lambda n: send(sc_send, sc_all.at[neg], sc_sem.at[0], sc_sem.at[1], (rep, n)),
    )
    sc_all[neg] = scores

    post_to(STOPS[2], 3)
    mates = ask_recv[rep].reshape(NEGS, 128).astype(BF16)
    halves = []
    for h in range(2):
        pick = bf(iota((32, NEGS), 0) // B + 8 * h == iota((32, NEGS), 1))
        wide = nn(pick, mates)
        at, t = iota((32, 128), 1), iota((32, 128), 0) % B
        halves.append(
            jnp.sum(
                jnp.where(at == 32 + t, wide * 32.0, 0.0) + jnp.where(at == 36 + t, wide, 0.0),
                axis=1,
                keepdims=True,
            )
        )
    positive = jnp.where(left, halves[0], halves[1])
    settle(sc_all.at[pl.ds(0, NEGS - 1)], sc_sem.at[1])

    def by_half(values):
        first = jnp.sum(jnp.where(left, values, 0.0), axis=1, keepdims=True)
        second = jnp.sum(jnp.where(left, 0.0, values), axis=1, keepdims=True)
        return jnp.where(left, first, second)

    all_scores = sc_all[...]
    shape = (NEGS, 32, 128)
    cand_id = (iota(shape, 0) * OWN + iota(shape, 2) % OWN).astype(F32)
    is_pos = cand_id == positive[None]
    pos_score = by_half(jnp.sum(jnp.where(is_pos, all_scores, 0.0), axis=0))
    gaps = all_scores - pos_score[None] + MARGIN
    small = jnp.exp(-jnp.abs(gaps))
    losses = jnp.maximum(gaps, 0.0) + jnp.log1p(small)
    sigmoid = jnp.where(gaps >= 0.0, 1.0, small) / (1.0 + small)
    loss = by_half(jnp.sum(losses, axis=0)) / (NEGS * OWN)
    totals = by_half(jnp.sum(sigmoid, axis=0))
    own_gap = sc_all[neg] - pos_score + MARGIN
    own_small = jnp.exp(-jnp.abs(own_gap))
    own_sig = jnp.where(own_gap >= 0.0, 1.0, own_small) / (1.0 + own_small)
    own_id = (neg * OWN + iota((32, 128), 1) % OWN).astype(F32)
    score_grad = (own_sig - jnp.where(own_id == positive, totals, 0.0)) / (NEGS * OWN)

    g_left = jnp.where(left, score_grad, 0.0).astype(BF16)
    g_right = jnp.where(left, 0.0, score_grad).astype(BF16)
    eg = jnp.concatenate([nn(g_left, cand_v[...]), nn(g_right, cand_v[...])], axis=0).astype(BF16)
    row_p, col_p = iota((256, 64), 0), iota((256, 64), 1)
    eg_out = jnp.zeros((256, part), F32)
    for c in range(4):
        move = bf((row_p // 16 == col_p // 4) & (row_p % 16 == 4 * c + col_p % 4))
        eg_out = eg_out + nn(move, eg[:, c * part : (c + 1) * part])
    eg_send[...] = eg_out.astype(BF16).reshape(NEGS, 16, part)
    around(
        neg, NEGS,
        lambda n: send(eg_send.at[n], eg_recv.at[neg], eg_sem.at[0], eg_sem.at[1], (rep, n)),
    )
    eg_recv[neg] = eg_send[neg]

    post_to(STOPS[3], 4)
    for b in range(8):
        curt_v[b % 2, 128 * (b // 2) : 128 * (b // 2) + 128, :] = (
            cur_v[:, 128 * b : 128 * b + 128].astype(F32).T.astype(BF16)
        )
    settle(eg_recv.at[pl.ds(0, NEGS - 1)], eg_sem.at[1])
    eg_sum = jnp.sum(eg_recv[...].astype(F32), axis=0)
    embed_grad = []
    for c in range(4):
        move = (
            (iota((8, 16), 1) == iota((8, 16), 0) + 4 * c) & (iota((8, 16), 0) < B)
        ).astype(F32)
        embed_grad.append(nn(move, eg_sum, HIGH))
    embed_grad = jnp.concatenate(embed_grad, axis=1)

    post_to(STOPS[4])

    top_grad = inv_top * embed_grad - top_in * (
        inv_top * inv_top * inv_top * jnp.mean(embed_grad * top_in, axis=1, keepdims=True)
    )
    normed_grad = tn(hop_mat, top_grad, HIGH)
    mixed_grad = inv_mid * normed_grad - mixed * (
        inv_mid * inv_mid * inv_mid * jnp.mean(normed_grad * mixed, axis=1, keepdims=True)
    )
    mixed_in_grad = jnp.where(mixed_in > 0.0, mixed_grad, 0.0).astype(BF16)
    total = jnp.zeros((HOP1, H), F32)
    for j in range(TILES):
        total = total + nt(mixed_in_grad[:, j * TILE : (j + 1) * TILE], cw_v[j, F : F + H, :])
    pooled_g[...] = total

    post_to(STOPS[5])

    def products(j, slot):
        spread_grad = jnp.broadcast_to(
            pooled_g[:, j * TILE : (j + 1) * TILE][:, None, :], (HOP1, SLOTS, TILE)
        ).reshape(REQ, TILE)
        pgrad_v[slot] = jnp.where(
            mask_v[j].astype(F32) > 0.0, spread_grad * weight, 0.0
        ).astype(BF16)
        p_send[j] = nn(curt_v[1 - core], pgrad_v[slot]).astype(BF16)
        send(p_send.at[j], p_recv.at[j], p_ssem.at[j], p_rsem.at[j], mate)
        p_own[j] = nn(curt_v[core], pgrad_v[slot])

    def pass_on(j):
        settle(p_recv.at[j], p_rsem.at[j])
        chip_sum = p_own[j] + p_recv[j].astype(F32)
        if j < 2:
            a1_send[j] = chip_sum.astype(BF16).reshape(YS, 128, TILE)
            around(
                y, YS,
                lambda q: send(
                    a1_send.at[j, q], a1_recv.at[j, y], a1_ssem.at[j], a1_rsem.at[j],
                    (q * CORES + core, neg),
                ),
            )
            a1_recv[j, y] = a1_send[j, y]
        else:
            k = j - 2
            for q in range(YS):
                b1_f[:, 8 * q : 8 * q + 8, :] = chip_sum[128 * q : 128 * q + 128].reshape(
                    NEGS, 8, TILE
                )
            b1_send[k] = b1_f[...].astype(BF16)
            around(
                neg, NEGS,
                lambda n: send(
                    b1_send.at[k, n], b1_recv.at[k, neg], b1_ssem.at[k], b1_rsem.at[k], (rep, n)
                ),
            )
            b1_recv[k, neg] = b1_send[k, neg]

    order = (0, 2, 1, 3)
    for step, j in enumerate(order):
        products(j, step % 2)
        if step > 0:
            pass_on(order[step - 1])
    pass_on(order[-1])
    post_to(STOPS[6])

    owner_col = cols_v[:, 0:1]
    rank_col = cols_v[:, 1:2]
    third = jnp.floor((rank_col + 0.5) * (1.0 / 3.0))
    left_over = rank_col - 3.0 * third
    slot_main = owner_col * 16.0 + rank_col
    slot_tail = [
        jnp.where(left_over == float(c), owner_col * 16.0 + 12.0 + third, -1.0) for c in range(3)
    ]

    def place(k):
        settle(row_recv.at[k, pl.ds(0, NEGS - 1 if k == 0 else NEGS)], row_rsem.at[k])
        block = row_recv[k].reshape(512, WIDE)
        line = (iota((REQ, 512), 1) + k * 512).astype(F32)
        body = nn(bf(line == slot_main), block)
        tail = jnp.zeros((REQ, PART), F32)
        for c in range(3):
            tail = tail + nn(bf(line == slot_tail[c]), block[:, c * PART : (c + 1) * PART])
        new = jnp.concatenate([body, tail], axis=1).astype(BF16)
        rows_acc[...] = new if k == 0 else rows_acc[...] + new

    lines = (iota((32, 128), 0) == iota((32, 128), 1) + B * (neg % 8)).astype(F32)
    half = jnp.where(neg // 8 == 0, 0, OWN)
    mine = tn(loss, lines, HIGH)
    loss_ref[...] = jnp.sum(
        jnp.where(iota((128, 128), 0) == half, mine, 0.0), axis=0, keepdims=True
    )[:, 0:B]
    cand_out[...] = tn(g_left, e_v[0:32, :])[0:OWN] + tn(g_right, e_v[32:64, :])[OWN:128]
    place(0)
    place(1)
    place(2)

    for j in range(2):
        settle(a1_recv.at[j, pl.ds(0, YS - 1)], a1_rsem.at[j])
        a2_f[:, 8 * j : 8 * j + 8, :] = jnp.sum(a1_recv[j].astype(F32), axis=0).reshape(
            NEGS, 8, TILE
        )
    a2_send[...] = a2_f[...].astype(BF16)
    around(
        neg, NEGS,
        lambda n: send(a2_send.at[n], a2_recv.at[neg], a2_sem.at[0], a2_sem.at[1], (rep, n)),
    )
    a2_recv[neg] = a2_send[neg]
    for k in range(2):
        settle(b1_recv.at[k, pl.ds(0, NEGS - 1)], b1_rsem.at[k])
        b2_f[:, 8 * k : 8 * k + 8, :] = jnp.sum(b1_recv[k].astype(F32), axis=0).reshape(
            YS, 8, TILE
        )
    b2_send[...] = b2_f[...].astype(BF16)
    around(
        y, YS,
        lambda q: send(
            b2_send.at[q], b2_recv.at[y], b2_sem.at[0], b2_sem.at[1], (q * CORES + core, neg)
        ),
    )
    b2_recv[y] = b2_send[y]

    post_to(STOPS[7])
    place(3)

    settle(a2_recv.at[pl.ds(0, NEGS - 1)], a2_sem.at[1])
    a_sum = jnp.sum(a2_recv[...].astype(F32), axis=0)
    settle(b2_recv.at[pl.ds(0, YS - 1)], b2_sem.at[1])
    b_sum = jnp.sum(b2_recv[...].astype(F32), axis=0)
    for j in range(2):
        ngrad_ref[:, j * TILE : (j + 1) * TILE] = a_sum[8 * j : 8 * j + 8]
        ngrad_ref[:, (j + 2) * TILE : (j + 3) * TILE] = b_sum[8 * j : 8 * j + 8]

    settle(ask_send.at[pl.ds(0, REPS - 1)], ask_sem.at[0])
    settle(ask_mid.at[:, pl.ds(0, NEGS - 1)], ask_sem.at[2])
    for k in range(YS):
        settle(row_out.at[k], out_ssem.at[k])
        settle(row_send.at[k, pl.ds(0, NEGS - 1 if k == 0 else NEGS)], row_ssem.at[k])
    settle(emb_all.at[pl.ds(0, NEGS - 1)], emb_sem.at[0])
    settle(sc_all.at[pl.ds(0, NEGS - 1)], sc_sem.at[0])
    settle(eg_send.at[pl.ds(0, NEGS - 1)], eg_sem.at[0])
    for j in range(TILES):
        settle(p_send.at[j], p_ssem.at[j])
    for j in range(2):
        settle(a1_send.at[j, pl.ds(0, YS - 1)], a1_ssem.at[j])
        settle(b1_send.at[j, pl.ds(0, NEGS - 1)], b1_ssem.at[j])
    settle(a2_send.at[pl.ds(0, NEGS - 1)], a2_sem.at[0])
    settle(b2_send.at[pl.ds(0, YS - 1)], b2_sem.at[0])


def local(
    feature_table, cur_rows, next_owner, next_local, slot_counts, hop_counts, positive_ids,
    neighbor_weight, combine_weight, candidates,
):
    vmem = pl.BlockSpec(memory_space=pltpu.VMEM)
    smem = pl.BlockSpec(memory_space=pltpu.SMEM)
    hbm = pl.BlockSpec(memory_space=pl.ANY)
    dma = pltpu.SemaphoreType.DMA
    part = H // 4
    scratch = [
        pltpu.VMEM((REQ, F), BF16),
        pltpu.VMEM((2, 512, REQ), BF16),
        pltpu.VMEM((F, F), BF16),
        pltpu.VMEM((TILES, F, TILE), BF16),
        pltpu.VMEM((TILES, F + H, TILE), BF16),
        pltpu.VMEM((2 * OWN, H), BF16),
        pltpu.VMEM((TILES, REQ, TILE), BF16),
        pltpu.VMEM((2, REQ, TILE), BF16),
        pltpu.VMEM((HOP1, F + H), BF16),
        pltpu.VMEM((HOP1, H), F32),
        pltpu.VMEM((HOP1, H), F32),
        pltpu.VMEM((REPS, NEGS, 1, 128), F32),
        pltpu.VMEM((REPS, NEGS, 1, 128), F32),
        pltpu.VMEM((REPS, NEGS, 1, 128), F32),
        pltpu.VMEM((DEVS, 128), F32),
        pltpu.VMEM((YS, NEGS, 16, WIDE), BF16),
        pltpu.VMEM((YS, NEGS, CORES, 16, WIDE), BF16),
        pltpu.VMEM((YS, NEGS, CORES, 16, WIDE), BF16),
        pltpu.VMEM((REQ, 16), F32),
        pltpu.VMEM((16, part), BF16),
        pltpu.VMEM((NEGS, 16, part), BF16),
        pltpu.VMEM((64, H), BF16),
        pltpu.VMEM((32, 128), F32),
        pltpu.VMEM((NEGS, 32, 128), F32),
        pltpu.VMEM((NEGS, 16, part), BF16),
        pltpu.VMEM((NEGS, 16, part), BF16),
        pltpu.VMEM((TILES, 512, TILE), BF16),
        pltpu.VMEM((TILES, 512, TILE), BF16),
        pltpu.VMEM((TILES, 512, TILE), F32),
        pltpu.VMEM((2, YS, 128, TILE), BF16),
        pltpu.VMEM((2, YS, 128, TILE), BF16),
        pltpu.VMEM((NEGS, 16, TILE), F32),
        pltpu.VMEM((NEGS, 16, TILE), BF16),
        pltpu.VMEM((NEGS, 16, TILE), BF16),
        pltpu.VMEM((NEGS, 32, TILE), F32),
        pltpu.VMEM((2, NEGS, 32, TILE), BF16),
        pltpu.VMEM((2, NEGS, 32, TILE), BF16),
        pltpu.VMEM((YS, 16, TILE), F32),
        pltpu.VMEM((YS, 16, TILE), BF16),
        pltpu.VMEM((YS, 16, TILE), BF16),
        dma((4 + 2 * TILES,)),
        dma((4,)), dma((YS,)), dma((YS,)), dma((YS,)), dma((YS,)),
        dma((2,)), dma((2,)), dma((2,)),
        dma((TILES,)), dma((TILES,)),
        dma((2,)), dma((2,)), dma((2,)),
        dma((2,)), dma((2,)), dma((2,)),
    ]
    next_rows, loss, cand_grad, neighbor_grad = pl.pallas_call(
        kernel,
        out_shape=(
            pltpu.VMEM((REQ, F), BF16),
            pltpu.VMEM((1, B), F32),
            pltpu.VMEM((OWN, H), F32),
            pltpu.VMEM((8, H), F32),
        ),
        in_specs=[vmem, vmem, vmem, vmem, smem, hbm, hbm, hbm, hbm, hbm],
        out_specs=(vmem, vmem, vmem, vmem),
        scratch_shapes=scratch,
        compiler_params=pltpu.CompilerParams(
            collective_id=0, has_side_effects=True, vmem_limit_bytes=58 * 2**20
        ),
        name="step",
    )(
        next_owner.reshape(1, REQ),
        next_local,
        slot_counts.T,
        hop_counts,
        positive_ids,
        feature_table,
        cur_rows,
        neighbor_weight,
        combine_weight,
        candidates,
    )
    return next_rows, loss.reshape(B), cand_grad, neighbor_grad


def solution(mesh):
    both = P(("rep", "neg"), None)
    flat = P(("rep", "neg"))
    return jax.shard_map(
        local,
        mesh=mesh,
        in_specs=(both, both, both, flat, both, both, flat, P(), P(), both),
        out_specs=(both, flat, both, both),
        check_vma=False,
    )
```
